32 devices in a mesh: row: 8 (over z, core), col: 4 (over y, x).
Axes of the slice: x: 2, y: 2, z: 4, core: 2. Of those that a mesh axis runs over, the one named last changes fastest.
Arguments:
- queries: bfloat16 [1536, 3072], P('row', 'col'), may hold values from -24 to 24
- keys_tile: bfloat16 [1536, 3072], P('row', 'col'), may hold values from -4.5 to 4.5
- values_tile: bfloat16 [1536, 3072], P('row', 'col'), may hold values from -6 to 6
- out_weight: bfloat16 [3072, 6144], P('row', 'col'), may hold values from -0.75 to 0.75
- out_grad: bfloat16 [1536, 6144], P('row', 'col'), may hold values from -1.5 to 1.5
Outputs:
- mixed: bfloat16 [1536, 6144], P('row', 'col')
- query_grad: bfloat16 [1536, 3072], P('row', 'col')
- key_grad: bfloat16 [1536, 3072], P('row', 'col')
- value_grad: bfloat16 [1536, 3072], P('row', 'col')
- weight_grad: bfloat16 [3072, 6144], P('row', 'col')
The draws below stay inside these ranges and needn't reach their ends.
All inputs are finite; a program needn't handle non-finite values.
Results may differ from the reference program's by a relative error of at most 0.019.
Values may be sent and summed in bfloat16 or wider, within the bound.
No kernel may reach another device: no remote copies, remote signals or barrier semaphores. Data moves between devices by JAX's collectives and lax.ppermute only.
A program may use at most 128 MiB of HBM per device.

```python
import jax
import jax.numpy as jnp
from jax import lax

D = 6144
HEADS = 24
HD = 128
TOKENS = 1536


def draw_pair(key):
    query_key = jax.random.fold_in(key, 101)
    key_key = jax.random.fold_in(key, 202)
    width = HEADS * HD
    keys_f = jnp.clip(jax.random.normal(key_key, (TOKENS, width), jnp.float32), -4.0, 4.0)
    queries_f = jnp.clip(2.0 * jax.random.normal(query_key, (TOKENS, width), jnp.float32), -8.0, 8.0)
    return (queries_f, keys_f)


def draw_queries(key, part):
    return draw_pair(key)[0].astype(jnp.bfloat16)


def draw_keys_tile(key, part):
    return draw_pair(key)[1].astype(jnp.bfloat16)


def block_levels(own_key, extent, pieces, least, top_value):
    gain, own = 1.0, jax.random.fold_in(own_key, 6)
    for position, parts in pieces:
        draws = jnp.exp(jax.random.uniform(jax.random.fold_in(own, position), (parts,), jnp.float32, least / len(pieces), top_value / len(pieces)))
        gain = gain * jnp.repeat(draws, extent[position] // parts).reshape([-1 if axis == position else 1 for axis in range(len(extent))])
    return gain


def centred(key, extent, deviation, limit, split=(), dtype=jnp.bfloat16):
    array = jax.random.normal(key, extent, jnp.float32) * deviation
    if len(split) > 0:
        array = block_levels(key, extent, split, -0.22, 0.18) * array
    return jnp.clip(array, min=-limit, max=limit).astype(dtype)


def setup_inputs(seed: int = 0) -> dict:
    key_of = jax.random.split(jax.random.key(seed), 6)
    queries = draw_queries(jax.random.fold_in(key_of[5], 71), 0)
    keys_tile = draw_keys_tile(jax.random.fold_in(key_of[5], 71), 0)
    values_tile = centred(key_of[2], (TOKENS, HEADS * HD), 1.0, 6.0, ((0, 8), (1, 4)))
    out_weight = centred(key_of[3], (HEADS * HD, D), (HD // 2) ** -0.5, 0.75, ((0, 8), (1, 4)))
    out_grad = centred(key_of[4], (TOKENS, D), 0.25, 1.5, ((0, 8), (1, 4)))
    return dict(queries=queries, keys_tile=keys_tile, values_tile=values_tile, out_weight=out_weight, out_grad=out_grad)


def head_forward(args):
    query_head, key_head, value_head = args
    scores = jnp.einsum("qd,kd->qk", query_head.astype(jnp.float32), key_head.astype(jnp.float32)) * (HD ** -0.5)
    top = jnp.max(scores, axis=1, keepdims=True)
    lse = top[:, 0] + jnp.log(jnp.sum(jnp.exp(scores - top), axis=1))
    probs = jnp.exp(scores - lse[:, None]).astype(jnp.bfloat16)
    attn = jnp.dot(probs, value_head, preferred_element_type=jnp.float32).astype(jnp.bfloat16)
    return attn, lse


def head_backward(args):
    query_head, key_head, value_head, grad_head, attn_head, lse = args
    delta = jnp.sum(grad_head.astype(jnp.float32) * attn_head.astype(jnp.float32), axis=1)
    scores = jnp.einsum("qd,kd->qk", query_head.astype(jnp.float32), key_head.astype(jnp.float32)) * (HD ** -0.5)
    probs = jnp.exp(scores - lse[:, None]).astype(jnp.bfloat16)
    dprob = jnp.einsum("qd,kd->qk", grad_head.astype(jnp.float32), value_head.astype(jnp.float32))
    dscore = (probs.astype(jnp.float32) * (dprob - delta[:, None]) * (HD ** -0.5)).astype(jnp.bfloat16)
    query_grad = jnp.dot(dscore, key_head, preferred_element_type=jnp.float32).astype(jnp.bfloat16)
    key_grad = jnp.dot(dscore.T, query_head, preferred_element_type=jnp.float32).astype(jnp.bfloat16)
    value_grad = jnp.dot(probs.T, grad_head, preferred_element_type=jnp.float32).astype(jnp.bfloat16)
    return query_grad, key_grad, value_grad


def split_heads(block):
    return block.reshape(block.shape[0], HEADS, HD).transpose(1, 0, 2)


def merge_heads(block):
    return block.transpose(1, 0, 2).reshape(block.shape[1], HEADS * HD)


def reference(queries, keys_tile, values_tile, out_weight, out_grad):
    query3 = split_heads(queries)
    key3 = split_heads(keys_tile)
    value3 = split_heads(values_tile)
    attn3, lse = lax.map(head_forward, (query3, key3, value3))
    attn = merge_heads(attn3)
    mixed = jnp.dot(attn, out_weight, preferred_element_type=jnp.float32).astype(jnp.bfloat16)
    d_attn = jnp.dot(out_grad, out_weight.T, preferred_element_type=jnp.float32).astype(jnp.bfloat16)
    weight_grad = jnp.dot(attn.T, out_grad, preferred_element_type=jnp.float32).astype(jnp.bfloat16)
    grad3 = split_heads(d_attn)
    query_g, key_g, value_g = lax.map(head_backward, (query3, key3, value3, grad3, attn3, lse))
    return mixed, merge_heads(query_g), merge_heads(key_g), merge_heads(value_g), weight_grad
```

```python
import functools

import jax
import jax.numpy as jnp
from jax import lax
from jax.experimental import pallas as pl
from jax.experimental.pallas import tpu as pltpu
from jax.sharding import PartitionSpec as P

HD = 128
SCALE = HD ** (-0.5)
LOG2E = 1.4426950408889634
F32 = jnp.float32
BF16 = jnp.bfloat16


def head_forward(args):
    query_head, key_head, value_head = args
    scores = jnp.einsum(
        "qd,kd->qk", query_head, key_head, preferred_element_type=jnp.float32
    ) * HD ** (-0.5)
    top = jnp.max(scores, axis=1, keepdims=True)
    lse = top[:, 0] + jnp.log(jnp.sum(jnp.exp(scores - top), axis=1))
    probs = jnp.exp(scores - lse[:, None]).astype(jnp.bfloat16)
    attn = jnp.dot(probs, value_head, preferred_element_type=jnp.float32).astype(jnp.bfloat16)
    return (attn, lse)


def score_grads(query_head, key_head, value_head, grad_head, lse, delta):
    scores = jnp.einsum(
        "qd,kd->qk", query_head, key_head, preferred_element_type=jnp.float32
    ) * HD ** (-0.5)
    probs = jnp.exp(scores - lse[:, None]).astype(jnp.bfloat16)
    dprob = jnp.einsum("qd,kd->qk", grad_head, value_head, preferred_element_type=jnp.float32)
    dscore = (probs.astype(jnp.float32) * (dprob - delta[:, None]) * HD ** (-0.5)).astype(
        jnp.bfloat16
    )
    return (probs, dscore)


def split_heads(block):
    return block.reshape(block.shape[0], block.shape[1] // HD, HD).transpose(1, 0, 2)


def merge_heads(block):
    return block.transpose(1, 0, 2).reshape(block.shape[1], block.shape[0] * HD)


def per_device(queries, keys_tile, values_tile, out_weight, out_grad):
    query3 = split_heads(queries)
    key_local = split_heads(keys_tile)
    value_local = split_heads(values_tile)
    key_every, value_every = (
        lax.all_gather(key_local, "row", axis=1, tiled=True),
        lax.all_gather(value_local, "row", axis=1, tiled=True),
    )
    attn3, lse = lax.map(head_forward, (query3, key_every, value_every))
    attn = merge_heads(attn3)
    attn_row = lax.all_gather(attn, "col", axis=1, tiled=True)
    weight_col = lax.all_gather(out_weight, "row", axis=0, tiled=True)
    mixed = jnp.dot(attn_row, weight_col, preferred_element_type=jnp.float32).astype(jnp.bfloat16)
    partial_grad = jnp.einsum("rc,fc->rf", out_grad, weight_col, preferred_element_type=jnp.float32)
    d_attn = lax.psum_scatter(partial_grad, "col", scatter_dimension=1, tiled=True).astype(
        jnp.bfloat16
    )
    weight_grad = lax.psum_scatter(
        jnp.einsum("rf,rc->fc", attn_row, out_grad, preferred_element_type=jnp.float32).astype(
            jnp.bfloat16
        ),
        "row",
        scatter_dimension=0,
        tiled=True,
    )
    grad3 = split_heads(d_attn)
    delta = jnp.sum(grad3.astype(jnp.float32) * attn3.astype(jnp.float32), axis=2)

    def head_backward(args):
        query_head, key_head, value_head, grad_head, lse_head, delta_head = args
        probs, dscore = score_grads(
            query_head, key_head, value_head, grad_head, lse_head, delta_head
        )
        query_g = jnp.dot(dscore, key_head, preferred_element_type=jnp.float32).astype(jnp.bfloat16)
        key_term = jnp.einsum("qk,qd->kd", dscore, query_head, preferred_element_type=jnp.float32)
        value_term = jnp.einsum("qk,qd->kd", probs, grad_head, preferred_element_type=jnp.float32)
        return (query_g, key_term, value_term)

    query_g3, key_terms, value_terms = lax.map(
        head_backward, (query3, key_every, value_every, grad3, lse, delta)
    )
    key_g3, value_g3 = (
        lax.psum_scatter(key_terms, "row", scatter_dimension=1, tiled=True),
        lax.psum_scatter(value_terms, "row", scatter_dimension=1, tiled=True),
    )
    key_g3 = key_g3.astype(jnp.bfloat16)
    value_g3 = value_g3.astype(jnp.bfloat16)
    return (mixed, merge_heads(query_g3), merge_heads(key_g3), merge_heads(value_g3), weight_grad)


PLANES, CORES, COLS = 4, 2, 4


def row_shift(s):
    return [
        (CORES * z + k, CORES * ((z + s) % PLANES) + k)
        for z in range(PLANES)
        for k in range(CORES)
    ]


SWAP = [(CORES * z + k, CORES * z + 1 - k) for z in range(PLANES) for k in range(CORES)]


def col_xor(j):
    return [(c, c ^ j) for c in range(COLS)]


def pick(stack, index):
    return lax.dynamic_index_in_dim(stack, index, 0, keepdims=False)


def nt(a, b):
    return lax.dot_general(a, b, (((1,), (1,)), ((), ())), preferred_element_type=F32)


def tn(a, b):
    return lax.dot_general(a, b, (((0,), (0,)), ((), ())), preferred_element_type=F32)


def forward_kernel(q_ref, k_ref, v_ref, p_ref, attn_ref):
    raw = nt(k_ref[0], q_ref[...])
    top = jnp.max(raw, axis=0, keepdims=True)
    e = jnp.exp2((raw - top) * (SCALE * LOG2E))
    total = jnp.sum(e, axis=0, keepdims=True)
    probs = (e * (1.0 / total)).astype(BF16)
    p_ref[0] = probs
    attn_ref[...] = tn(v_ref[0], probs).T.astype(BF16)


def attention_forward(q, k, v):
    rows, keys = q.shape[0] // 3, k.shape[1]
    return pl.pallas_call(
        forward_kernel,
        grid=(3,),
        in_specs=[
            pl.BlockSpec((rows, HD), lambda i: (i, 0)),
            pl.BlockSpec((1, keys, HD), lambda i: (i // 2, 0, 0)),
            pl.BlockSpec((1, keys, HD), lambda i: (i // 2, 0, 0)),
        ],
        out_specs=[
            pl.BlockSpec((1, keys, rows), lambda i: (i, 0, 0)),
            pl.BlockSpec((rows, HD), lambda i: (i, 0)),
        ],
        out_shape=[
            jax.ShapeDtypeStruct((3, keys, rows), BF16),
            jax.ShapeDtypeStruct((3 * rows, HD), BF16),
        ],
        compiler_params=pltpu.CompilerParams(vmem_limit_bytes=40 * 2**20),
        cost_estimate=pl.CostEstimate(
            flops=3 * 4 * rows * keys * HD,
            bytes_accessed=3 * rows * keys * 2,
            transcendentals=3 * rows * keys,
        ),
        name="attention_forward",
    )(q, k, v)


def backward_kernel(q_ref, k_ref, v_ref, p_ref, attn_ref, grad_ref, dq_ref, dk_ref, dv_ref):
    step = pl.program_id(0)
    grad = grad_ref[...]
    product = grad.astype(F32) * attn_ref[...].astype(F32)
    delta = jnp.sum(product.T, axis=0, keepdims=True)
    probs = p_ref[0]
    dprob = nt(v_ref[0], grad)
    dscore = (probs.astype(F32) * (dprob - delta) * SCALE).astype(BF16)
    dq_ref[...] = tn(k_ref[0], dscore).T.astype(BF16)
    dk = jnp.dot(dscore, q_ref[...], preferred_element_type=F32)
    dv = jnp.dot(probs, grad, preferred_element_type=F32)

    @pl.when(step != 1)
    def _():
        dk_ref[0] = dk
        dv_ref[0] = dv

    @pl.when(step == 1)
    def _():
        dk_ref[0] += dk
        dv_ref[0] += dv


def attention_backward(q, k, v, probs, attn, grad):
    rows, keys = q.shape[0] // 3, k.shape[1]
    by_query = pl.BlockSpec((rows, HD), lambda i: (i, 0))
    by_head = pl.BlockSpec((1, keys, HD), lambda i: (i // 2, 0, 0))
    return pl.pallas_call(
        backward_kernel,
        grid=(3,),
        in_specs=[
            by_query,
            by_head,
            by_head,
            pl.BlockSpec((1, keys, rows), lambda i: (i, 0, 0)),
            by_query,
            by_query,
        ],
        out_specs=[by_query, by_head, by_head],
        out_shape=[
            jax.ShapeDtypeStruct(q.shape, BF16),
            jax.ShapeDtypeStruct(k.shape, F32),
            jax.ShapeDtypeStruct(k.shape, F32),
        ],
        compiler_params=pltpu.CompilerParams(vmem_limit_bytes=48 * 2**20),
        cost_estimate=pl.CostEstimate(
            flops=3 * 8 * rows * keys * HD,
            bytes_accessed=3 * rows * keys * 2,
            transcendentals=0,
        ),
        name="attention_backward",
    )(q, k, v, probs, attn, grad)


def per_device_fast(queries, keys_tile, values_tile, out_weight, out_grad):
    tokens = queries.shape[0]
    half = tokens // 2
    row, col = lax.axis_index("row"), lax.axis_index("col")
    plane, core = row // CORES, row % CORES

    def head(block, g):
        return block[:, g * HD : (g + 1) * HD]

    def spread(pieces):
        return [pick(pieces, col)] + [
            lax.ppermute(pick(pieces, col ^ j), "col", col_xor(j)) for j in range(1, COLS)
        ]

    def input_piece(d):
        y, x = divmod(d, 2)
        a, b = 3 * y + x, 3 * y + 2
        return jnp.concatenate(
            [
                head(queries, a),
                head(queries, b)[x * half : (x + 1) * half],
                head(keys_tile, a),
                head(keys_tile, b),
                head(values_tile, a),
                head(values_tile, b),
            ]
        )

    over_col = jnp.stack(spread(jnp.stack([input_piece(d) for d in range(COLS)])))
    arrived = [pick(over_col, col ^ plane)]
    for s in range(1, PLANES):
        arrived.append(
            lax.ppermute(pick(over_col, col ^ ((plane + s) % PLANES)), "row", row_shift(s))
        )
    arrived = jnp.stack(arrived)

    grads = [out_grad]
    for s in range(1, PLANES):
        grads.append(lax.ppermute(grads[-1], "row", row_shift(1)))
    grads_own = jnp.concatenate(grads)
    grads_other = jnp.concatenate([lax.ppermute(g, "row", SWAP) for g in grads])
    weight_other = lax.ppermute(out_weight, "row", SWAP)
    weight = jnp.where(
        core == 0,
        jnp.concatenate([out_weight, weight_other]),
        jnp.concatenate([weight_other, out_weight]),
    )

    q = jnp.concatenate(
        [
            arrived[:, :tokens].reshape(PLANES * tokens, HD),
            arrived[:, tokens : tokens + half].reshape(PLANES * half, HD),
        ]
    )
    kv_own = arrived[:, tokens + half :].reshape(PLANES, 4, tokens, HD).transpose(1, 0, 2, 3)
    kv_own = kv_own.reshape(4, PLANES * tokens, HD)
    kv = jnp.concatenate([kv_own, lax.ppermute(kv_own, "row", SWAP)], axis=1)
    k, v = kv[:2], kv[2:]
    probs, attn = attention_forward(q, k, v)

    attn_col = jnp.stack([attn] + [lax.ppermute(attn, "col", col_xor(j)) for j in range(1, COLS)])
    by_col = [pick(attn_col, col ^ d) for d in range(COLS)]
    columns = []
    for y in range(2):
        columns += [by_col[2 * y][: PLANES * tokens], by_col[2 * y + 1][: PLANES * tokens]]
        halves = [by_col[2 * y + x][PLANES * tokens :].reshape(PLANES, half, HD) for x in range(2)]
        columns.append(jnp.concatenate(halves, axis=1).reshape(PLANES * tokens, HD))
    attn_plane = jnp.concatenate(columns, axis=1)

    def term(s):
        block = attn_plane[s * tokens : (s + 1) * tokens]
        return jnp.dot(block, weight, preferred_element_type=F32)

    moving = term(1).astype(BF16)
    for s in range(2, PLANES + 1):
        moving = lax.ppermute(moving, "row", row_shift(1)).astype(F32) + term(s % PLANES)
        moving = moving.astype(BF16)
    mixed = moving

    d_part = nt(grads_own, weight).astype(BF16)

    def grad_piece(d):
        y, x = divmod(d, 2)
        b = head(d_part, 3 * y + 2).reshape(PLANES, 2, half, HD)[:, x]
        return jnp.concatenate([head(d_part, 3 * y + x), b.reshape(PLANES * half, HD)])

    d_terms = spread(jnp.stack([grad_piece(d) for d in range(COLS)]))
    d_attn = sum(t.astype(F32) for t in d_terms).astype(BF16)

    width = out_weight.shape[0]
    attn_own = lax.dynamic_slice_in_dim(attn_plane, core * width, width, 1)
    attn_sent = lax.dynamic_slice_in_dim(attn_plane, (1 - core) * width, width, 1)
    attn_other = lax.ppermute(attn_sent, "row", SWAP)
    weight_grad = (tn(attn_own, grads_own) + tn(attn_other, grads_other)).astype(BF16)

    dq, dk, dv = attention_backward(q, k, v, probs, attn, d_attn)
    dkv = jnp.concatenate([dk, dv])
    own = PLANES * tokens
    dkv = dkv[:, :own] + lax.ppermute(dkv[:, own:].astype(BF16), "row", SWAP).astype(F32)
    dkv = dkv.astype(BF16).reshape(4, PLANES, tokens, HD)
    dq_a = dq[:own].reshape(PLANES, tokens, HD)
    dq_b = dq[own:].reshape(PLANES, half, HD)
    home = [jnp.concatenate([dq_a[s], dq_b[s]] + [dkv[i, s] for i in range(4)]) for s in range(PLANES)]
    home = jnp.stack(
        home[:1] + [lax.ppermute(home[s], "row", row_shift(-s)) for s in range(1, PLANES)]
    )
    back = [pick(home, (col - plane) % PLANES)] + [
        lax.ppermute(pick(home, ((col ^ j) - plane) % PLANES), "col", col_xor(j))
        for j in range(1, COLS)
    ]
    back = jnp.stack(back)
    back = [pick(back, col ^ d) for d in range(COLS)]
    outs = [[], [], []]
    for y in range(2):
        left, right = back[2 * y], back[2 * y + 1]
        outs[0] += [
            left[:tokens],
            right[:tokens],
            jnp.concatenate([left[tokens : tokens + half], right[tokens : tokens + half]]),
        ]
        for i in range(2):
            at = tokens + half + 2 * i * tokens
            b = left[at + tokens : at + 2 * tokens].astype(F32) + right[at + tokens : at + 2 * tokens].astype(F32)
            outs[1 + i] += [left[at : at + tokens], right[at : at + tokens], b.astype(BF16)]
    query_g, key_g, value_g = [jnp.concatenate(o, axis=1) for o in outs]
    return (mixed, query_g, key_g, value_g, weight_grad)


def solution(mesh):
    spec = P("row", "col")
    fast = mesh.shape["row"] == PLANES * CORES and mesh.shape["col"] == COLS

    def run(queries, keys_tile, values_tile, out_weight, out_grad):
        heads = queries.shape[1] // HD
        fits = fast and heads == 6 * COLS and queries.shape[0] % (32 * mesh.shape["row"]) == 0
        return jax.shard_map(
            per_device_fast if fits else per_device,
            mesh=mesh,
            in_specs=(spec,) * 5,
            out_specs=(spec,) * 5,
            check_vma=False,
        )(queries, keys_tile, values_tile, out_weight, out_grad)

    return run
```

```python
import functools

import jax
import jax.numpy as jnp
from jax import lax
from jax.experimental import pallas as pl
from jax.experimental.pallas import tpu as pltpu
from jax.sharding import PartitionSpec as P

HD = 128
SCALE = HD ** (-0.5)
LOG2E = 1.4426950408889634
F32 = jnp.float32
BF16 = jnp.bfloat16


def head_forward(args):
    query_head, key_head, value_head = args
    scores = jnp.einsum(
        "qd,kd->qk", query_head, key_head, preferred_element_type=jnp.float32
    ) * HD ** (-0.5)
    top = jnp.max(scores, axis=1, keepdims=True)
    lse = top[:, 0] + jnp.log(jnp.sum(jnp.exp(scores - top), axis=1))
    probs = jnp.exp(scores - lse[:, None]).astype(jnp.bfloat16)
    attn = jnp.dot(probs, value_head, preferred_element_type=jnp.float32).astype(jnp.bfloat16)
    return (attn, lse)


def score_grads(query_head, key_head, value_head, grad_head, lse, delta):
    scores = jnp.einsum(
        "qd,kd->qk", query_head, key_head, preferred_element_type=jnp.float32
    ) * HD ** (-0.5)
    probs = jnp.exp(scores - lse[:, None]).astype(jnp.bfloat16)
    dprob = jnp.einsum("qd,kd->qk", grad_head, value_head, preferred_element_type=jnp.float32)
    dscore = (probs.astype(jnp.float32) * (dprob - delta[:, None]) * HD ** (-0.5)).astype(
        jnp.bfloat16
    )
    return (probs, dscore)


def split_heads(block):
    return block.reshape(block.shape[0], block.shape[1] // HD, HD).transpose(1, 0, 2)


def merge_heads(block):
    return block.transpose(1, 0, 2).reshape(block.shape[1], block.shape[0] * HD)


def per_device(queries, keys_tile, values_tile, out_weight, out_grad):
    query3 = split_heads(queries)
    key_local = split_heads(keys_tile)
    value_local = split_heads(values_tile)
    key_every, value_every = (
        lax.all_gather(key_local, "row", axis=1, tiled=True),
        lax.all_gather(value_local, "row", axis=1, tiled=True),
    )
    attn3, lse = lax.map(head_forward, (query3, key_every, value_every))
    attn = merge_heads(attn3)
    attn_row = lax.all_gather(attn, "col", axis=1, tiled=True)
    weight_col = lax.all_gather(out_weight, "row", axis=0, tiled=True)
    mixed = jnp.dot(attn_row, weight_col, preferred_element_type=jnp.float32).astype(jnp.bfloat16)
    partial_grad = jnp.einsum("rc,fc->rf", out_grad, weight_col, preferred_element_type=jnp.float32)
    d_attn = lax.psum_scatter(partial_grad, "col", scatter_dimension=1, tiled=True).astype(
        jnp.bfloat16
    )
    weight_grad = lax.psum_scatter(
        jnp.einsum("rf,rc->fc", attn_row, out_grad, preferred_element_type=jnp.float32).astype(
            jnp.bfloat16
        ),
        "row",
        scatter_dimension=0,
        tiled=True,
    )
    grad3 = split_heads(d_attn)
    delta = jnp.sum(grad3.astype(jnp.float32) * attn3.astype(jnp.float32), axis=2)

    def head_backward(args):
        query_head, key_head, value_head, grad_head, lse_head, delta_head = args
        probs, dscore = score_grads(
            query_head, key_head, value_head, grad_head, lse_head, delta_head
        )
        query_g = jnp.dot(dscore, key_head, preferred_element_type=jnp.float32).astype(jnp.bfloat16)
        key_term = jnp.einsum("qk,qd->kd", dscore, query_head, preferred_element_type=jnp.float32)
        value_term = jnp.einsum("qk,qd->kd", probs, grad_head, preferred_element_type=jnp.float32)
        return (query_g, key_term, value_term)

    query_g3, key_terms, value_terms = lax.map(
        head_backward, (query3, key_every, value_every, grad3, lse, delta)
    )
    key_g3, value_g3 = (
        lax.psum_scatter(key_terms, "row", scatter_dimension=1, tiled=True),
        lax.psum_scatter(value_terms, "row", scatter_dimension=1, tiled=True),
    )
    key_g3 = key_g3.astype(jnp.bfloat16)
    value_g3 = value_g3.astype(jnp.bfloat16)
    return (mixed, merge_heads(query_g3), merge_heads(key_g3), merge_heads(value_g3), weight_grad)


PLANES, CORES, COLS = 4, 2, 4
ORDER = (0, 1, 3, 2)


def row_shift(s):
    return [
        (CORES * z + k, CORES * ((z + s) % PLANES) + k)
        for z in range(PLANES)
        for k in range(CORES)
    ]


SWAP = [(CORES * z + k, CORES * z + 1 - k) for z in range(PLANES) for k in range(CORES)]


def col_xor(j):
    return [(c, c ^ j) for c in range(COLS)]


def pick(stack, index):
    return lax.dynamic_index_in_dim(stack, index, 0, keepdims=False)


def nt(a, b):
    return lax.dot_general(a, b, (((1,), (1,)), ((), ())), preferred_element_type=F32)


def tn(a, b):
    return lax.dot_general(a, b, (((0,), (0,)), ((), ())), preferred_element_type=F32)


def forward_kernel(q_ref, k_ref, v_ref, p_ref, attn_ref):
    raw = nt(k_ref[0], q_ref[...])
    top = jnp.max(raw, axis=0, keepdims=True)
    e = jnp.exp2((raw - top) * (SCALE * LOG2E))
    total = jnp.sum(e, axis=0, keepdims=True)
    probs = (e * (1.0 / total)).astype(BF16)
    p_ref[0] = probs
    attn_ref[...] = tn(v_ref[0], probs).T.astype(BF16)


def attention_forward(q, k, v):
    rows, keys = q.shape[0] // 3, k.shape[1]
    return pl.pallas_call(
        forward_kernel,
        grid=(3,),
        in_specs=[
            pl.BlockSpec((rows, HD), lambda i: (i, 0)),
            pl.BlockSpec((1, keys, HD), lambda i: (i // 2, 0, 0)),
            pl.BlockSpec((1, keys, HD), lambda i: (i // 2, 0, 0)),
        ],
        out_specs=[
            pl.BlockSpec((1, keys, rows), lambda i: (i, 0, 0)),
            pl.BlockSpec((rows, HD), lambda i: (i, 0)),
        ],
        out_shape=[
            jax.ShapeDtypeStruct((3, keys, rows), BF16),
            jax.ShapeDtypeStruct((3 * rows, HD), BF16),
        ],
        compiler_params=pltpu.CompilerParams(vmem_limit_bytes=16 * 2**20),
        name="attention_forward",
    )(q, k, v)


def backward_kernel(
    q_ref, k_ref, v_ref, p_ref, attn_ref, grad_ref, dq_ref, own_ref, other_ref, sums_ref
):
    step = pl.program_id(0)
    grad = grad_ref[...]
    product = grad.astype(F32) * attn_ref[...].astype(F32)
    delta = jnp.sum(product.T, axis=0, keepdims=True)
    probs = p_ref[0]
    dprob = nt(v_ref[0], grad)
    dscore = (probs.astype(F32) * (dprob - delta) * SCALE).astype(BF16)
    dq_ref[...] = tn(k_ref[0], dscore).T.astype(BF16)
    dk = jnp.dot(dscore, q_ref[...], preferred_element_type=F32)
    dv = jnp.dot(probs, grad, preferred_element_type=F32)

    @pl.when(step == 0)
    def _():
        sums_ref[0] = dk
        sums_ref[1] = dv

    @pl.when(step != 0)
    def _():
        half = dk.shape[0] // 2
        for i, new in enumerate((dk, dv)):
            new = jnp.where(step == 1, sums_ref[i], 0.0) + new
            own_ref[i, 0] = new[:half]
            other_ref[i, 0] = new[half:].astype(BF16)


def attention_backward(q, k, v, probs, attn, grad):
    rows, keys = q.shape[0] // 3, k.shape[1]
    by_query = pl.BlockSpec((rows, HD), lambda i: (i, 0))
    by_head = pl.BlockSpec((1, keys, HD), lambda i: (i // 2, 0, 0))
    by_half = pl.BlockSpec((2, 1, keys // 2, HD), lambda i: (0, i // 2, 0, 0))
    return pl.pallas_call(
        backward_kernel,
        grid=(3,),
        in_specs=[
            by_query,
            by_head,
            by_head,
            pl.BlockSpec((1, keys, rows), lambda i: (i, 0, 0)),
            by_query,
            by_query,
        ],
        out_specs=[by_query, by_half, by_half],
        out_shape=[
            jax.ShapeDtypeStruct(q.shape, BF16),
            jax.ShapeDtypeStruct((2, 2, keys // 2, HD), F32),
            jax.ShapeDtypeStruct((2, 2, keys // 2, HD), BF16),
        ],
        scratch_shapes=[pltpu.VMEM((2, keys, HD), F32)],
        compiler_params=pltpu.CompilerParams(vmem_limit_bytes=20 * 2**20),
        name="attention_backward",
    )(q, k, v, probs, attn, grad)


def pack_kernel(q_ref, k_ref, v_ref, *out_refs):
    tokens = q_ref.shape[0]
    half = tokens // 2
    col = lax.axis_index("col")
    for j, out_ref in enumerate(out_refs):
        to = lax.bitwise_xor(col, j)
        y, x = lax.div(to, 2), lax.rem(to, 2)
        a = pl.ds(pl.multiple_of((3 * y + x) * HD, HD), HD)
        b = pl.ds(pl.multiple_of((3 * y + 2) * HD, HD), HD)
        at = tokens + half
        out_ref[:tokens] = q_ref[:, a]
        out_ref[tokens:at] = q_ref[pl.ds(pl.multiple_of(x * half, half), half), b]
        for i, block in enumerate((k_ref[:, a], k_ref[:, b], v_ref[:, a], v_ref[:, b])):
            out_ref[at + i * tokens : at + (i + 1) * tokens] = block


def pack(queries, keys, values):
    tokens = queries.shape[0]
    piece = jax.ShapeDtypeStruct((tokens // 2 + 5 * tokens, HD), BF16)
    return pl.pallas_call(
        pack_kernel,
        out_shape=[piece] * COLS,
        cost_estimate=pl.CostEstimate(flops=0, bytes_accessed=6 * queries.size, transcendentals=0),
        name="pack_inputs",
    )(queries, keys, values)


def after(value, *earlier):
    return lax.optimization_barrier((value, earlier))[0]


def per_device_fast(queries, keys_tile, values_tile, out_weight, out_grad):
    tokens = queries.shape[0]
    half = tokens // 2
    own = PLANES * tokens
    width = out_weight.shape[0]
    row, col = lax.axis_index("row"), lax.axis_index("col")
    plane, core = row // CORES, row % CORES

    def head(block, g):
        return block[:, g * HD : (g + 1) * HD]

    def to_col(block, j):
        return lax.ppermute(block, "col", col_xor(j))

    def to_plane(block, s):
        return lax.ppermute(block, "row", row_shift(s))

    def swap(block):
        return lax.ppermute(block, "row", SWAP)

    grad_1 = to_plane(out_grad, 1)
    grad_3 = to_plane(out_grad, -1)
    weight_other = swap(out_weight)

    pieces = pack(queries, keys_tile, values_tile)
    over_col = jnp.stack([pieces[0]] + [to_col(pieces[j], j) for j in (1, 2, 3)])
    over_col = after(over_col, grad_1, grad_3)
    arrived = [pick(over_col, col ^ plane)]
    for s in ORDER[1:]:
        arrived.append(to_plane(pick(over_col, col ^ ((plane + s) % PLANES)), s))
    arrived = jnp.stack(arrived)
    weight = jnp.where(
        core == 0,
        jnp.concatenate([out_weight, weight_other]),
        jnp.concatenate([weight_other, out_weight]),
    )

    def grad_pieces(*blocks):
        part = jnp.concatenate([nt(g, weight).astype(BF16) for g in blocks])
        rows = part.shape[0]

        def piece(d):
            y, x = divmod(d, 2)
            b = head(part, 3 * y + 2).reshape(rows // tokens, 2, half, HD)[:, x]
            return jnp.concatenate([head(part, 3 * y + x), b.reshape(rows // 2, HD)])

        every = jnp.stack([piece(d) for d in range(COLS)])
        return [pick(every, col ^ j) for j in range(COLS)]

    def sum_over_col(sent):
        terms = sent[:1] + [to_col(sent[j], j) for j in (1, 2, 3)]
        return sum(t.astype(F32) for t in terms).astype(BF16)

    early = grad_pieces(out_grad, grad_1, grad_3)
    d_attn_early = sum_over_col(early)
    arrived = after(arrived, early)

    q = jnp.concatenate(
        [
            arrived[:, :tokens].reshape(own, HD),
            arrived[:, tokens : tokens + half].reshape(PLANES * half, HD),
        ]
    )
    kv_own = arrived[:, tokens + half :].reshape(PLANES, 4, tokens, HD).transpose(1, 0, 2, 3)
    kv_own = kv_own.reshape(4, own, HD)
    kv = [jnp.concatenate([kv_own[i], swap(kv_own[i])]) for i in range(4)]
    k, v = jnp.stack(kv[:2]), jnp.stack(kv[2:])

    grad_2 = to_plane(after(grad_1, arrived), 1)
    grads = [out_grad, grad_1, grad_3, grad_2]

    probs, attn = attention_forward(q, k, v)

    def plane_heads(a, b):
        sent = jnp.concatenate([a, b])
        every = jnp.stack([sent] + [to_col(sent, j) for j in (1, 2, 3)])
        by_col = [pick(every, col ^ d) for d in range(COLS)]
        rows = a.shape[0]
        columns = []
        for y in range(2):
            columns += [by_col[2 * y][:rows], by_col[2 * y + 1][:rows]]
            halves = [by_col[2 * y + x][rows:].reshape(-1, half, HD) for x in range(2)]
            columns.append(jnp.concatenate(halves, axis=1).reshape(rows, HD))
        return jnp.concatenate(columns, axis=1)

    attn_a, attn_b = attn[:own], attn[own:]
    heads_2 = plane_heads(attn_a[3 * tokens :], attn_b[3 * half :])
    heads_rest = plane_heads(attn_a[: 3 * tokens], attn_b[: 3 * half])
    attn_plane = jnp.concatenate([heads_rest, heads_2])

    def term(s):
        block = heads_2 if s == 2 else heads_rest[ORDER.index(s) * tokens :][:tokens]
        return jnp.dot(block, weight, preferred_element_type=F32)

    late = grad_pieces(after(grad_2, attn))
    d_attn_late = sum_over_col(late)
    mixed_2 = to_plane(term(2).astype(BF16), 1)
    mixed_1 = to_plane(after(term(1).astype(BF16), mixed_2), -1)

    d_attn = jnp.concatenate(
        [
            d_attn_early[: 3 * tokens],
            d_attn_late[:tokens],
            d_attn_early[3 * tokens :],
            d_attn_late[tokens:],
        ]
    )
    dq, dkv, dkv_other = attention_backward(q, k, v, probs, attn, d_attn)
    dkv_other = jnp.stack([jnp.stack([swap(dkv_other[i, h]) for h in range(2)]) for i in range(2)])
    dkv = dkv + dkv_other.astype(F32)
    dkv = dkv.astype(BF16).reshape(4, PLANES, tokens, HD)
    dq_a = dq[:own].reshape(PLANES, tokens, HD)
    dq_b = dq[own:].reshape(PLANES, half, HD)
    home = [
        jnp.concatenate([dq_a[p], dq_b[p]] + [dkv[i, p] for i in range(4)])
        for p in (ORDER.index(s) for s in range(PLANES))
    ]
    home, mixed_2, mixed_1 = after((home, mixed_2, mixed_1))

    attn_own = lax.dynamic_slice_in_dim(attn_plane, core * width, width, 1)
    attn_sent = lax.dynamic_slice_in_dim(attn_plane, (1 - core) * width, width, 1)
    attn_other = swap(attn_sent)
    grads_own = jnp.concatenate(grads)
    grads_other = jnp.concatenate([swap(g) for g in grads])
    weight_grad = (
        tn(after(attn_own, home), grads_own) + tn(attn_other, grads_other)
    ).astype(BF16)

    home = jnp.stack(home[:1] + [to_plane(home[s], -s) for s in range(1, PLANES)])

    term_3 = (mixed_2.astype(F32) + term(3)).astype(BF16)
    base = term(0) + mixed_1.astype(F32)
    term_3, base = after((term_3, base), home)
    mixed_3 = to_plane(term_3, 1)

    back = [pick(home, (col - plane) % PLANES)] + [
        to_col(pick(home, ((col ^ j) - plane) % PLANES), j) for j in (1, 2, 3)
    ]
    back = jnp.stack(back)
    back = [pick(back, col ^ d) for d in range(COLS)]
    outs = [[], [], []]
    for y in range(2):
        left, right = back[2 * y], back[2 * y + 1]
        outs[0] += [
            left[:tokens],
            right[:tokens],
            jnp.concatenate([left[tokens : tokens + half], right[tokens : tokens + half]]),
        ]
        for i in range(2):
            at = tokens + half + 2 * i * tokens
            to = at + tokens
            b = left[to : to + tokens].astype(F32) + right[to : to + tokens].astype(F32)
            outs[1 + i] += [left[at:to], right[at:to], b.astype(BF16)]
    query_g, key_g, value_g = [jnp.concatenate(o, axis=1) for o in outs]
    mixed = (base + mixed_3.astype(F32)).astype(BF16)
    return (mixed, query_g, key_g, value_g, weight_grad)


def solution(mesh):
    spec = P("row", "col")
    fast = mesh.shape["row"] == PLANES * CORES and mesh.shape["col"] == COLS

    def run(queries, keys_tile, values_tile, out_weight, out_grad):
        heads = queries.shape[1] // HD
        fits = fast and heads == 6 * COLS and queries.shape[0] % (32 * mesh.shape["row"]) == 0
        return jax.shard_map(
            per_device_fast if fits else per_device,
            mesh=mesh,
            in_specs=(spec,) * 5,
            out_specs=(spec,) * 5,
            check_vma=False,
        )(queries, keys_tile, values_tile, out_weight, out_grad)

    return run
```

```python
import functools

import jax
import jax.numpy as jnp
from jax import lax
from jax.experimental import pallas as pl
from jax.experimental.pallas import tpu as pltpu
from jax.sharding import PartitionSpec as P

HD = 128
SCALE = HD ** (-0.5)
LOG2E = 1.4426950408889634
F32 = jnp.float32
BF16 = jnp.bfloat16


def head_forward(args):
    query_head, key_head, value_head = args
    scores = jnp.einsum(
        "qd,kd->qk", query_head, key_head, preferred_element_type=jnp.float32
    ) * HD ** (-0.5)
    top = jnp.max(scores, axis=1, keepdims=True)
    lse = top[:, 0] + jnp.log(jnp.sum(jnp.exp(scores - top), axis=1))
    probs = jnp.exp(scores - lse[:, None]).astype(jnp.bfloat16)
    attn = jnp.dot(probs, value_head, preferred_element_type=jnp.float32).astype(jnp.bfloat16)
    return (attn, lse)


def score_grads(query_head, key_head, value_head, grad_head, lse, delta):
    scores = jnp.einsum(
        "qd,kd->qk", query_head, key_head, preferred_element_type=jnp.float32
    ) * HD ** (-0.5)
    probs = jnp.exp(scores - lse[:, None]).astype(jnp.bfloat16)
    dprob = jnp.einsum("qd,kd->qk", grad_head, value_head, preferred_element_type=jnp.float32)
    dscore = (probs.astype(jnp.float32) * (dprob - delta[:, None]) * HD ** (-0.5)).astype(
        jnp.bfloat16
    )
    return (probs, dscore)


def split_heads(block):
    return block.reshape(block.shape[0], block.shape[1] // HD, HD).transpose(1, 0, 2)


def merge_heads(block):
    return block.transpose(1, 0, 2).reshape(block.shape[1], block.shape[0] * HD)


def per_device(queries, keys_tile, values_tile, out_weight, out_grad):
    query3 = split_heads(queries)
    key_local = split_heads(keys_tile)
    value_local = split_heads(values_tile)
    key_every, value_every = (
        lax.all_gather(key_local, "row", axis=1, tiled=True),
        lax.all_gather(value_local, "row", axis=1, tiled=True),
    )
    attn3, lse = lax.map(head_forward, (query3, key_every, value_every))
    attn = merge_heads(attn3)
    attn_row = lax.all_gather(attn, "col", axis=1, tiled=True)
    weight_col = lax.all_gather(out_weight, "row", axis=0, tiled=True)
    mixed = jnp.dot(attn_row, weight_col, preferred_element_type=jnp.float32).astype(jnp.bfloat16)
    partial_grad = jnp.einsum("rc,fc->rf", out_grad, weight_col, preferred_element_type=jnp.float32)
    d_attn = lax.psum_scatter(partial_grad, "col", scatter_dimension=1, tiled=True).astype(
        jnp.bfloat16
    )
    weight_grad = lax.psum_scatter(
        jnp.einsum("rf,rc->fc", attn_row, out_grad, preferred_element_type=jnp.float32).astype(
            jnp.bfloat16
        ),
        "row",
        scatter_dimension=0,
        tiled=True,
    )
    grad3 = split_heads(d_attn)
    delta = jnp.sum(grad3.astype(jnp.float32) * attn3.astype(jnp.float32), axis=2)

    def head_backward(args):
        query_head, key_head, value_head, grad_head, lse_head, delta_head = args
        probs, dscore = score_grads(
            query_head, key_head, value_head, grad_head, lse_head, delta_head
        )
        query_g = jnp.dot(dscore, key_head, preferred_element_type=jnp.float32).astype(jnp.bfloat16)
        key_term = jnp.einsum("qk,qd->kd", dscore, query_head, preferred_element_type=jnp.float32)
        value_term = jnp.einsum("qk,qd->kd", probs, grad_head, preferred_element_type=jnp.float32)
        return (query_g, key_term, value_term)

    query_g3, key_terms, value_terms = lax.map(
        head_backward, (query3, key_every, value_every, grad3, lse, delta)
    )
    key_g3, value_g3 = (
        lax.psum_scatter(key_terms, "row", scatter_dimension=1, tiled=True),
        lax.psum_scatter(value_terms, "row", scatter_dimension=1, tiled=True),
    )
    key_g3 = key_g3.astype(jnp.bfloat16)
    value_g3 = value_g3.astype(jnp.bfloat16)
    return (mixed, merge_heads(query_g3), merge_heads(key_g3), merge_heads(value_g3), weight_grad)


PLANES, CORES, COLS = 4, 2, 4
ORDER = (0, 1, 3, 2)
WINDOW = pl.CostEstimate(flops=4 * 10**10, bytes_accessed=0, transcendentals=0)
SMALL = pl.CostEstimate(flops=10**6, bytes_accessed=10**3, transcendentals=0)


def row_shift(s):
    return [
        (CORES * z + k, CORES * ((z + s) % PLANES) + k)
        for z in range(PLANES)
        for k in range(CORES)
    ]


SWAP = [(CORES * z + k, CORES * z + 1 - k) for z in range(PLANES) for k in range(CORES)]


def col_xor(j):
    return [(c, c ^ j) for c in range(COLS)]


def pick(stack, index):
    return lax.dynamic_index_in_dim(stack, index, 0, keepdims=False)


def nt(a, b):
    return lax.dot_general(a, b, (((1,), (1,)), ((), ())), preferred_element_type=F32)


def tn(a, b):
    return lax.dot_general(a, b, (((0,), (0,)), ((), ())), preferred_element_type=F32)


def forward_kernel(q_ref, k_ref, v_ref, p_ref, attn_ref):
    raw = nt(k_ref[0], q_ref[...])
    top = jnp.max(raw, axis=0, keepdims=True)
    e = jnp.exp2((raw - top) * (SCALE * LOG2E))
    total = jnp.sum(e, axis=0, keepdims=True)
    probs = (e * (1.0 / total)).astype(BF16)
    p_ref[0] = probs
    attn_ref[...] = tn(v_ref[0], probs).T.astype(BF16)


def attention_forward(q, k, v):
    rows, keys = q.shape[0] // 3, k.shape[1]
    return pl.pallas_call(
        forward_kernel,
        grid=(3,),
        in_specs=[
            pl.BlockSpec((rows, HD), lambda i: (i, 0)),
            pl.BlockSpec((1, keys, HD), lambda i: (i // 2, 0, 0)),
            pl.BlockSpec((1, keys, HD), lambda i: (i // 2, 0, 0)),
        ],
        out_specs=[
            pl.BlockSpec((1, keys, rows), lambda i: (i, 0, 0)),
            pl.BlockSpec((rows, HD), lambda i: (i, 0)),
        ],
        out_shape=[
            pltpu.HBM((3, keys, rows), BF16),
            jax.ShapeDtypeStruct((3 * rows, HD), BF16),
        ],
        compiler_params=pltpu.CompilerParams(vmem_limit_bytes=16 * 2**20),
        cost_estimate=WINDOW,
        name="attention_forward",
    )(q, k, v)


def backward_kernel(
    q_ref, k_ref, v_ref, p_ref, attn_ref, early_ref, *refs
):
    late_refs, (dq_ref, own_ref, other_ref, grad_ref, sums_ref) = refs[:COLS], refs[COLS:]
    step = pl.program_id(0)
    rows = q_ref.shape[0]

    @pl.when(step == 0)
    def _():
        early_a, late_a = early_ref.shape[0] * 2 // 3, late_refs[0].shape[0] * 2 // 3
        late = sum(ref[...].astype(F32) for ref in late_refs).astype(BF16)
        own = early_a + late_a
        grad_ref[:early_a] = early_ref[:early_a]
        grad_ref[early_a:own] = late[:late_a]
        grad_ref[own : own + early_a // 2] = early_ref[early_a:]
        grad_ref[own + early_a // 2 :] = late[late_a:]

    grad = grad_ref[pl.ds(pl.multiple_of(step * rows, rows), rows)]
    product = grad.astype(F32) * attn_ref[...].astype(F32)
    delta = jnp.sum(product.T, axis=0, keepdims=True)
    probs = p_ref[0]
    dprob = nt(v_ref[0], grad)
    dscore = (probs.astype(F32) * (dprob - delta) * SCALE).astype(BF16)
    dq_ref[...] = tn(k_ref[0], dscore).T.astype(BF16)
    dk = jnp.dot(dscore, q_ref[...], preferred_element_type=F32)
    dv = jnp.dot(probs, grad, preferred_element_type=F32)

    @pl.when(step == 0)
    def _():
        sums_ref[0] = dk
        sums_ref[1] = dv

    @pl.when(step != 0)
    def _():
        half = dk.shape[0] // 2
        for i, new in enumerate((dk, dv)):
            new = jnp.where(step == 1, sums_ref[i], 0.0) + new
            own_ref[i, 0] = new[:half]
            other_ref[i, 0] = new[half:].astype(BF16)


def attention_backward(q, k, v, probs, attn, early, late):
    rows, keys = q.shape[0] // 3, k.shape[1]
    by_query = pl.BlockSpec((rows, HD), lambda i: (i, 0))
    by_head = pl.BlockSpec((1, keys, HD), lambda i: (i // 2, 0, 0))
    by_half = pl.BlockSpec((2, 1, keys // 2, HD), lambda i: (0, i // 2, 0, 0))
    return pl.pallas_call(
        backward_kernel,
        grid=(3,),
        in_specs=[
            by_query,
            by_head,
            by_head,
            pl.BlockSpec((1, keys, rows), lambda i: (i, 0, 0)),
            by_query,
            *[pl.BlockSpec(block.shape, lambda i: (0, 0)) for block in (early, *late)],
        ],
        out_specs=[by_query, by_half, by_half],
        out_shape=[
            jax.ShapeDtypeStruct(q.shape, BF16),
            jax.ShapeDtypeStruct((2, 2, keys // 2, HD), F32),
            jax.ShapeDtypeStruct((2, 2, keys // 2, HD), BF16),
        ],
        scratch_shapes=[pltpu.VMEM(q.shape, BF16), pltpu.VMEM((2, keys, HD), F32)],
        compiler_params=pltpu.CompilerParams(vmem_limit_bytes=20 * 2**20),
        cost_estimate=WINDOW,
        name="attention_backward",
    )(q, k, v, probs, attn, early, *late)


def pack_kernel(q_ref, k_ref, v_ref, *out_refs):
    tokens = q_ref.shape[0]
    half = tokens // 2
    col = lax.axis_index("col")
    for j, out_ref in enumerate(out_refs):
        to = lax.bitwise_xor(col, j)
        y, x = lax.div(to, 2), lax.rem(to, 2)
        a = pl.ds(pl.multiple_of((3 * y + x) * HD, HD), HD)
        b = pl.ds(pl.multiple_of((3 * y + 2) * HD, HD), HD)
        at = tokens + half
        out_ref[:tokens] = q_ref[:, a]
        out_ref[tokens:at] = q_ref[pl.ds(pl.multiple_of(x * half, half), half), b]
        for i, block in enumerate((k_ref[:, a], k_ref[:, b], v_ref[:, a], v_ref[:, b])):
            out_ref[at + i * tokens : at + (i + 1) * tokens] = block


def pack(queries, keys, values):
    tokens = queries.shape[0]
    piece = jax.ShapeDtypeStruct((tokens // 2 + 5 * tokens, HD), BF16)
    return pl.pallas_call(
        pack_kernel,
        out_shape=[piece] * COLS,
        cost_estimate=WINDOW,
        name="pack_inputs",
    )(queries, keys, values)


def grad_kernel(*refs):
    n = len(refs) - 2 - COLS - 1
    own_ref, other_ref = refs[n : n + 2]
    out_refs, part_ref = refs[n + 2 : -1], refs[-1]
    tokens = refs[0].shape[0]
    half = tokens // 2
    core, col = lax.rem(lax.axis_index("row"), CORES), lax.axis_index("col")
    for i in range(n):
        rows = pl.ds(i * tokens, tokens)
        block = refs[i][...]
        part_ref[core, rows] = nt(block, own_ref[...]).astype(BF16)
        part_ref[1 - core, rows] = nt(block, other_ref[...]).astype(BF16)
    for j, out_ref in enumerate(out_refs):
        to = lax.bitwise_xor(col, j)
        y, x = lax.div(to, 2), lax.rem(to, 2)
        out_ref[: n * tokens] = part_ref[y, :, pl.ds(pl.multiple_of(x * HD, HD), HD)]
        for i in range(n):
            rows = pl.ds(pl.multiple_of(i * tokens + x * half, half), half)
            out_ref[pl.ds(n * tokens + i * half, half)] = part_ref[y, rows, 2 * HD : 3 * HD]


def grad_pieces(blocks, own, other, cost=WINDOW):
    rows = len(blocks) * blocks[0].shape[0]
    piece = jax.ShapeDtypeStruct((rows + rows // 2, HD), BF16)
    return pl.pallas_call(
        grad_kernel,
        out_shape=[piece] * COLS,
        scratch_shapes=[pltpu.VMEM((CORES, rows, own.shape[0]), BF16)],
        compiler_params=pltpu.CompilerParams(vmem_limit_bytes=20 * 2**20),
        cost_estimate=cost,
        name="grad_pieces",
    )(*blocks, own, other)


def group(ref, index):
    width = ref.shape[1] // CORES
    return ref[:, pl.ds(pl.multiple_of(index * width, width), width)]


def term_kernel(block_ref, own_ref, other_ref, out_ref):
    core = lax.rem(lax.axis_index("row"), CORES)
    out = jnp.dot(group(block_ref, core), own_ref[...], preferred_element_type=F32)
    out += jnp.dot(group(block_ref, 1 - core), other_ref[...], preferred_element_type=F32)
    out_ref[...] = out.astype(out_ref.dtype)


def mixed_term(block, own, other, dtype, cost=SMALL):
    return pl.pallas_call(
        term_kernel,
        out_shape=jax.ShapeDtypeStruct((block.shape[0], own.shape[1]), dtype),
        compiler_params=pltpu.CompilerParams(vmem_limit_bytes=20 * 2**20),
        cost_estimate=cost,
        name="mixed_term",
    )(block, own, other)


def weight_grad_kernel(n, *refs):
    head_refs, grad_refs, total_refs, out_ref = refs[:n], refs[n : 2 * n], refs[2 * n : -1], refs[-1]
    width = out_ref.shape[1] // 4
    for i in range(4):
        columns = pl.ds(i * width, width)
        total = sum(tn(h[...], g[:, columns]) for h, g in zip(head_refs, grad_refs))
        for total_ref in total_refs:
            total = total + total_ref[:, columns].astype(F32)
        out_ref[:, columns] = total.astype(BF16)


def weight_grad_part(heads, grads, *total):
    return pl.pallas_call(
        functools.partial(weight_grad_kernel, len(heads)),
        out_shape=jax.ShapeDtypeStruct((heads[0].shape[1], grads[0].shape[1]), BF16),
        compiler_params=pltpu.CompilerParams(vmem_limit_bytes=28 * 2**20),
        cost_estimate=WINDOW,
        name="weight_grad",
    )(*heads, *grads, *total)


def join_kernel(*refs):
    in_refs, (q_ref, kv_ref) = refs[:PLANES], refs[PLANES:]
    tokens = kv_ref.shape[1] // PLANES
    half = tokens // 2
    for p, in_ref in enumerate(in_refs):
        q_ref[p * tokens : (p + 1) * tokens] = in_ref[:tokens]
        at = PLANES * tokens + p * half
        q_ref[at : at + half] = in_ref[tokens : tokens + half]
        for i in range(4):
            at = tokens + half + i * tokens
            kv_ref[i, p * tokens : (p + 1) * tokens] = in_ref[at : at + tokens]


def join(blocks, tokens):
    return pl.pallas_call(
        join_kernel,
        out_shape=[
            jax.ShapeDtypeStruct((PLANES * (tokens + tokens // 2), HD), BF16),
            jax.ShapeDtypeStruct((4, PLANES * tokens, HD), BF16),
        ],
        cost_estimate=SMALL,
        name="join",
    )(*blocks)


def fence_kernel(in_ref, out_ref):
    del in_ref, out_ref


def fence(*earlier):
    mark = lax.optimization_barrier((jnp.zeros((8, 128), F32), earlier))[0]
    return pl.pallas_call(
        fence_kernel,
        in_specs=[pl.BlockSpec(memory_space=pl.ANY)],
        out_specs=pl.BlockSpec(memory_space=pl.ANY),
        out_shape=jax.ShapeDtypeStruct(mark.shape, mark.dtype),
        input_output_aliases={0: 0},
        compiler_params=pltpu.CompilerParams(has_side_effects=True),
        cost_estimate=WINDOW,
        name="fence",
    )(mark)


def after(value, *earlier):
    return lax.optimization_barrier((value, earlier))[0]


def per_device_fast(queries, keys_tile, values_tile, out_weight, out_grad):
    tokens = queries.shape[0]
    half = tokens // 2
    own = PLANES * tokens
    width = out_weight.shape[0]
    row, col = lax.axis_index("row"), lax.axis_index("col")
    plane, core = row // CORES, row % CORES

    def head(block, g):
        return block[:, g * HD : (g + 1) * HD]

    def to_col(block, j):
        return lax.ppermute(block, "col", col_xor(j))

    def to_plane(block, s):
        return lax.ppermute(block, "row", row_shift(s))

    def swap(block):
        return lax.ppermute(block, "row", SWAP)

    grad_1 = to_plane(out_grad, 1)
    grad_3 = to_plane(out_grad, -1)
    weights = (out_weight, swap(out_weight))

    pieces = pack(*after((queries, keys_tile, values_tile), fence()))
    pieces = after(pieces, weights[1])
    moved = after([to_col(pieces[j], j) for j in (1, 2, 3)], fence(pieces))
    over_col = jnp.stack([pieces[0], *moved])

    def add_up(*terms):
        return sum(t.astype(F32) for t in terms).astype(BF16)

    arrived = [pick(over_col, col ^ plane)]
    for s in ORDER[1:]:
        arrived.append(to_plane(pick(over_col, col ^ ((plane + s) % PLANES)), s))
    early = grad_pieces((out_grad, grad_1, grad_3), *weights)
    early_sent = [to_col(early[j], j) for j in (1, 2)]
    early_sent.append(to_col(after(early[3], arrived[1]), 3))

    arrived = after(arrived, early)
    q, kv = join(arrived, tokens)
    kv = jnp.concatenate([kv, swap(kv)], axis=1)
    k, v = kv[:2], kv[2:]

    grad_2 = to_plane(after(grad_1, arrived), 1)
    grads = [out_grad, grad_1, grad_3, grad_2]

    probs, attn = attention_forward(q, k, v)
    grad_2 = after(grad_2, attn)
    d_attn_early = add_up(early[0], *after(early_sent, attn))

    def plane_heads(rows, every):
        by_col = [pick(every, col ^ d) for d in range(COLS)]
        columns = []
        for y in range(2):
            columns += [by_col[2 * y][:rows], by_col[2 * y + 1][:rows]]
            halves = [by_col[2 * y + x][rows:].reshape(-1, half, HD) for x in range(2)]
            columns.append(jnp.concatenate(halves, axis=1).reshape(rows, HD))
        return jnp.concatenate(columns, axis=1)

    attn_a, attn_b = attn[:own], attn[own:]
    sent = jnp.concatenate([attn_a[3 * tokens :], attn_b[3 * half :]])
    got = after([to_col(sent, j) for j in (1, 2, 3)], grad_2)
    heads_2 = plane_heads(tokens, jnp.stack([sent, *got]))
    term_2 = mixed_term(heads_2, *weights, BF16)
    mixed_2 = to_plane(term_2, 1)
    late = grad_pieces((after(grad_2, term_2),), *weights)
    late = [late[0]] + [to_col(late[j], j) for j in (1, 2, 3)]
    sent = jnp.concatenate([attn_a[: 3 * tokens], attn_b[: 3 * half]])
    pair = jnp.stack([sent, to_col(sent, 1)])
    rest = [pair, to_col(pair, 2)]

    dq, dkv, dkv_other = attention_backward(q, k, v, probs, attn, d_attn_early, late)
    rest, mixed_2 = after((rest, mixed_2), dq)

    dkv_other = jnp.stack([jnp.stack([swap(dkv_other[i, h]) for h in range(2)]) for i in range(2)])
    dkv = dkv + dkv_other.astype(F32)
    dkv = dkv.astype(BF16).reshape(4, PLANES, tokens, HD)
    dq_a = dq[:own].reshape(PLANES, tokens, HD)
    dq_b = dq[own:].reshape(PLANES, half, HD)
    home = [
        jnp.concatenate([dq_a[p], dq_b[p]] + [dkv[i, p] for i in range(4)])
        for p in (ORDER.index(s) for s in range(PLANES))
    ]

    away = [to_plane(home[s], -s) for s in range(1, PLANES)]

    heads_rest = plane_heads(3 * tokens, jnp.concatenate(rest))
    heads = [heads_rest[p * tokens : (p + 1) * tokens] for p in range(3)] + [heads_2]
    ours, theirs = [
        [lax.dynamic_slice_in_dim(h, g * width, width, 1) for h in heads] for g in (core, 1 - core)
    ]
    total = weight_grad_part(after(theirs, home), grads)

    head_0, head_1, head_3 = after(heads[:3], total)
    term_1 = mixed_term(head_1, *weights, BF16)
    mixed_1 = to_plane(term_1, -1)
    term_3 = (mixed_2.astype(F32) + mixed_term(head_3, *weights, F32)).astype(BF16)
    total = swap(total)
    term_0 = mixed_term(after(head_0, term_1, term_3), *weights, F32, WINDOW)

    away, mixed_1, total = after((away, mixed_1, total), term_0)
    home = [home[0], *away]
    weight_grad = weight_grad_part(after(ours, home), grads, total)

    mixed_3 = to_plane(after(term_3, home), 1)

    home = jnp.stack(home)
    back = [pick(home, (col - plane) % PLANES)] + [
        to_col(pick(home, ((col ^ j) - plane) % PLANES), j) for j in (1, 2, 3)
    ]
    back, mixed_3 = after((back, mixed_3), weight_grad)
    back = jnp.stack(back)
    back = [pick(back, col ^ d) for d in range(COLS)]
    outs = [[], [], []]
    for y in range(2):
        left, right = back[2 * y], back[2 * y + 1]
        outs[0] += [
            left[:tokens],
            right[:tokens],
            jnp.concatenate([left[tokens : tokens + half], right[tokens : tokens + half]]),
        ]
        for i in range(2):
            at = tokens + half + 2 * i * tokens
            to = at + tokens
            b = left[to : to + tokens].astype(F32) + right[to : to + tokens].astype(F32)
            outs[1 + i] += [left[at:to], right[at:to], b.astype(BF16)]
    query_g, key_g, value_g = [jnp.concatenate(o, axis=1) for o in outs]
    mixed = (term_0 + mixed_1.astype(F32) + mixed_3.astype(F32)).astype(BF16)
    return (mixed, query_g, key_g, value_g, weight_grad)


def solution(mesh):
    spec = P("row", "col")
    fast = mesh.shape["row"] == PLANES * CORES and mesh.shape["col"] == COLS

    def run(queries, keys_tile, values_tile, out_weight, out_grad):
        heads = queries.shape[1] // HD
        fits = fast and heads == 6 * COLS and queries.shape[0] % (32 * mesh.shape["row"]) == 0
        return jax.shard_map(
            per_device_fast if fits else per_device,
            mesh=mesh,
            in_specs=(spec,) * 5,
            out_specs=(spec,) * 5,
            check_vma=False,
        )(queries, keys_tile, values_tile, out_weight, out_grad)

    return run
```

```python
import functools

import jax
import jax.numpy as jnp
from jax import lax
from jax.experimental import pallas as pl
from jax.experimental.pallas import tpu as pltpu
from jax.sharding import PartitionSpec as P

HD = 128
SCALE = HD ** (-0.5)
LOG2E = 1.4426950408889634
F32 = jnp.float32
BF16 = jnp.bfloat16


def head_forward(args):
    query_head, key_head, value_head = args
    scores = jnp.einsum(
        "qd,kd->qk", query_head, key_head, preferred_element_type=jnp.float32
    ) * HD ** (-0.5)
    top = jnp.max(scores, axis=1, keepdims=True)
    lse = top[:, 0] + jnp.log(jnp.sum(jnp.exp(scores - top), axis=1))
    probs = jnp.exp(scores - lse[:, None]).astype(jnp.bfloat16)
    attn = jnp.dot(probs, value_head, preferred_element_type=jnp.float32).astype(jnp.bfloat16)
    return (attn, lse)


def score_grads(query_head, key_head, value_head, grad_head, lse, delta):
    scores = jnp.einsum(
        "qd,kd->qk", query_head, key_head, preferred_element_type=jnp.float32
    ) * HD ** (-0.5)
    probs = jnp.exp(scores - lse[:, None]).astype(jnp.bfloat16)
    dprob = jnp.einsum("qd,kd->qk", grad_head, value_head, preferred_element_type=jnp.float32)
    dscore = (probs.astype(jnp.float32) * (dprob - delta[:, None]) * HD ** (-0.5)).astype(
        jnp.bfloat16
    )
    return (probs, dscore)


def split_heads(block):
    return block.reshape(block.shape[0], block.shape[1] // HD, HD).transpose(1, 0, 2)


def merge_heads(block):
    return block.transpose(1, 0, 2).reshape(block.shape[1], block.shape[0] * HD)


def per_device(queries, keys_tile, values_tile, out_weight, out_grad):
    query3 = split_heads(queries)
    key_local = split_heads(keys_tile)
    value_local = split_heads(values_tile)
    key_every, value_every = (
        lax.all_gather(key_local, "row", axis=1, tiled=True),
        lax.all_gather(value_local, "row", axis=1, tiled=True),
    )
    attn3, lse = lax.map(head_forward, (query3, key_every, value_every))
    attn = merge_heads(attn3)
    attn_row = lax.all_gather(attn, "col", axis=1, tiled=True)
    weight_col = lax.all_gather(out_weight, "row", axis=0, tiled=True)
    mixed = jnp.dot(attn_row, weight_col, preferred_element_type=jnp.float32).astype(jnp.bfloat16)
    partial_grad = jnp.einsum("rc,fc->rf", out_grad, weight_col, preferred_element_type=jnp.float32)
    d_attn = lax.psum_scatter(partial_grad, "col", scatter_dimension=1, tiled=True).astype(
        jnp.bfloat16
    )
    weight_grad = lax.psum_scatter(
        jnp.einsum("rf,rc->fc", attn_row, out_grad, preferred_element_type=jnp.float32).astype(
            jnp.bfloat16
        ),
        "row",
        scatter_dimension=0,
        tiled=True,
    )
    grad3 = split_heads(d_attn)
    delta = jnp.sum(grad3.astype(jnp.float32) * attn3.astype(jnp.float32), axis=2)

    def head_backward(args):
        query_head, key_head, value_head, grad_head, lse_head, delta_head = args
        probs, dscore = score_grads(
            query_head, key_head, value_head, grad_head, lse_head, delta_head
        )
        query_g = jnp.dot(dscore, key_head, preferred_element_type=jnp.float32).astype(jnp.bfloat16)
        key_term = jnp.einsum("qk,qd->kd", dscore, query_head, preferred_element_type=jnp.float32)
        value_term = jnp.einsum("qk,qd->kd", probs, grad_head, preferred_element_type=jnp.float32)
        return (query_g, key_term, value_term)

    query_g3, key_terms, value_terms = lax.map(
        head_backward, (query3, key_every, value_every, grad3, lse, delta)
    )
    key_g3, value_g3 = (
        lax.psum_scatter(key_terms, "row", scatter_dimension=1, tiled=True),
        lax.psum_scatter(value_terms, "row", scatter_dimension=1, tiled=True),
    )
    key_g3 = key_g3.astype(jnp.bfloat16)
    value_g3 = value_g3.astype(jnp.bfloat16)
    return (mixed, merge_heads(query_g3), merge_heads(key_g3), merge_heads(value_g3), weight_grad)


PLANES, CORES, COLS = 4, 2, 4
ORDER = (0, 1, 3, 2)
WINDOW = pl.CostEstimate(flops=4 * 10**10, bytes_accessed=0, transcendentals=0)
SMALL = pl.CostEstimate(flops=10**6, bytes_accessed=10**3, transcendentals=0)


def row_shift(s):
    return [
        (CORES * z + k, CORES * ((z + s) % PLANES) + k)
        for z in range(PLANES)
        for k in range(CORES)
    ]


SWAP = [(CORES * z + k, CORES * z + 1 - k) for z in range(PLANES) for k in range(CORES)]


def col_xor(j):
    return [(c, c ^ j) for c in range(COLS)]


def pick(stack, index):
    return lax.dynamic_index_in_dim(stack, index, 0, keepdims=False)


def nt(a, b):
    return lax.dot_general(a, b, (((1,), (1,)), ((), ())), preferred_element_type=F32)


def tn(a, b):
    return lax.dot_general(a, b, (((0,), (0,)), ((), ())), preferred_element_type=F32)


def forward_kernel(*refs):
    own_refs, other_refs, (p_ref, attn_ref, q_ref, k_ref, v_ref) = refs[:PLANES], refs[PLANES:-5], refs[-5:]
    step = pl.program_id(0)
    rows = attn_ref.shape[0]

    @pl.when(step == 0)
    def _():
        tokens = k_ref.shape[1] // (2 * PLANES)
        half = tokens // 2
        for p, own_ref in enumerate(own_refs):
            q_ref[p * tokens : (p + 1) * tokens] = own_ref[:tokens]
            at = PLANES * tokens + p * half
            q_ref[at : at + half] = own_ref[tokens : tokens + half]
        for p, in_ref in enumerate(own_refs + other_refs):
            for i in range(4):
                at = tokens + half + i * tokens
                out_ref = (k_ref, v_ref)[i // 2]
                out_ref[i % 2, p * tokens : (p + 1) * tokens] = in_ref[at : at + tokens]

    head = lax.div(step, 2)
    raw = nt(k_ref[head], q_ref[pl.ds(pl.multiple_of(step * rows, rows), rows)])
    top = jnp.max(raw, axis=0, keepdims=True)
    e = jnp.exp2((raw - top) * (SCALE * LOG2E))
    total = jnp.sum(e, axis=0, keepdims=True)
    probs = (e * (1.0 / total)).astype(BF16)
    p_ref[0] = probs
    attn_ref[...] = tn(v_ref[head], probs).T.astype(BF16)


def attention_forward(own, other, tokens):
    rows, keys = 2 * tokens, 2 * PLANES * tokens

    def whole(*shape):
        return pl.BlockSpec(shape, lambda i: (0,) * len(shape))

    return pl.pallas_call(
        forward_kernel,
        grid=(3,),
        in_specs=[whole(*own[0].shape)] * (2 * PLANES),
        out_specs=[
            pl.BlockSpec((1, keys, rows), lambda i: (i, 0, 0)),
            pl.BlockSpec((rows, HD), lambda i: (i, 0)),
            whole(3 * rows, HD),
            whole(2, keys, HD),
            whole(2, keys, HD),
        ],
        out_shape=[
            pltpu.HBM((3, keys, rows), BF16),
            jax.ShapeDtypeStruct((3 * rows, HD), BF16),
            jax.ShapeDtypeStruct((3 * rows, HD), BF16),
            jax.ShapeDtypeStruct((2, keys, HD), BF16),
            jax.ShapeDtypeStruct((2, keys, HD), BF16),
        ],
        compiler_params=pltpu.CompilerParams(vmem_limit_bytes=24 * 2**20),
        cost_estimate=WINDOW,
        name="attention_forward",
    )(*own, *other)


def backward_kernel(
    q_ref, k_ref, v_ref, p_ref, attn_ref, *refs
):
    early_refs, late_refs, refs = refs[:COLS], refs[COLS : 2 * COLS], refs[2 * COLS :]
    dq_ref, own_ref, other_ref, grad_ref, sums_ref = refs
    step = pl.program_id(0)
    rows = q_ref.shape[0]

    @pl.when(step == 0)
    def _():
        early_a, late_a = early_refs[0].shape[0] * 2 // 3, late_refs[0].shape[0] * 2 // 3
        early = sum(ref[...].astype(F32) for ref in early_refs).astype(BF16)
        late = sum(ref[...].astype(F32) for ref in late_refs).astype(BF16)
        own = early_a + late_a
        grad_ref[:early_a] = early[:early_a]
        grad_ref[early_a:own] = late[:late_a]
        grad_ref[own : own + early_a // 2] = early[early_a:]
        grad_ref[own + early_a // 2 :] = late[late_a:]

    grad = grad_ref[pl.ds(pl.multiple_of(step * rows, rows), rows)]
    product = grad.astype(F32) * attn_ref[...].astype(F32)
    delta = jnp.sum(product.T, axis=0, keepdims=True)
    probs = p_ref[0]
    dprob = nt(v_ref[0], grad)
    dscore = (probs.astype(F32) * (dprob - delta) * SCALE).astype(BF16)
    dq_ref[...] = tn(k_ref[0], dscore).T.astype(BF16)
    dk = jnp.dot(dscore, q_ref[...], preferred_element_type=F32)
    dv = jnp.dot(probs, grad, preferred_element_type=F32)

    @pl.when(step == 0)
    def _():
        sums_ref[0] = dk
        sums_ref[1] = dv

    @pl.when(step != 0)
    def _():
        half = dk.shape[0] // 2
        for i, new in enumerate((dk, dv)):
            new = jnp.where(step == 1, sums_ref[i], 0.0) + new
            own_ref[i, 0] = new[:half]
            other_ref[i, 0] = new[half:].astype(BF16)


def attention_backward(q, k, v, probs, attn, early, late):
    rows, keys = q.shape[0] // 3, k.shape[1]
    by_query = pl.BlockSpec((rows, HD), lambda i: (i, 0))
    by_head = pl.BlockSpec((1, keys, HD), lambda i: (i // 2, 0, 0))
    by_half = pl.BlockSpec((2, 1, keys // 2, HD), lambda i: (0, i // 2, 0, 0))
    return pl.pallas_call(
        backward_kernel,
        grid=(3,),
        in_specs=[
            by_query,
            by_head,
            by_head,
            pl.BlockSpec((1, keys, rows), lambda i: (i, 0, 0)),
            by_query,
            *[pl.BlockSpec(block.shape, lambda i: (0, 0)) for block in (*early, *late)],
        ],
        out_specs=[by_query, by_half, by_half],
        out_shape=[
            jax.ShapeDtypeStruct(q.shape, BF16),
            jax.ShapeDtypeStruct((2, 2, keys // 2, HD), F32),
            jax.ShapeDtypeStruct((2, 2, keys // 2, HD), BF16),
        ],
        scratch_shapes=[pltpu.VMEM(q.shape, BF16), pltpu.VMEM((2, keys, HD), F32)],
        compiler_params=pltpu.CompilerParams(vmem_limit_bytes=20 * 2**20),
        cost_estimate=WINDOW,
        name="attention_backward",
    )(q, k, v, probs, attn, *early, *late)


def pack_kernel(q_ref, k_ref, v_ref, *out_refs):
    tokens = q_ref.shape[0]
    half = tokens // 2
    col = lax.axis_index("col")
    for j, out_ref in enumerate(out_refs):
        to = lax.bitwise_xor(col, j)
        y, x = lax.div(to, 2), lax.rem(to, 2)
        a = pl.ds(pl.multiple_of((3 * y + x) * HD, HD), HD)
        b = pl.ds(pl.multiple_of((3 * y + 2) * HD, HD), HD)
        at = tokens + half
        out_ref[:tokens] = q_ref[:, a]
        out_ref[tokens:at] = q_ref[pl.ds(pl.multiple_of(x * half, half), half), b]
        for i, block in enumerate((k_ref[:, a], k_ref[:, b], v_ref[:, a], v_ref[:, b])):
            out_ref[at + i * tokens : at + (i + 1) * tokens] = block


def pack(queries, keys, values):
    tokens = queries.shape[0]
    piece = jax.ShapeDtypeStruct((tokens // 2 + 5 * tokens, HD), BF16)
    return pl.pallas_call(
        pack_kernel,
        out_shape=[piece] * COLS,
        cost_estimate=WINDOW,
        name="pack_inputs",
    )(queries, keys, values)


def grad_kernel(*refs):
    n = len(refs) - 2 - COLS - 1
    own_ref, other_ref = refs[n : n + 2]
    out_refs, part_ref = refs[n + 2 : -1], refs[-1]
    tokens = refs[0].shape[0]
    half = tokens // 2
    core, col = lax.rem(lax.axis_index("row"), CORES), lax.axis_index("col")
    for i in range(n):
        rows = pl.ds(i * tokens, tokens)
        block = refs[i][...]
        part_ref[core, rows] = nt(block, own_ref[...]).astype(BF16)
        part_ref[1 - core, rows] = nt(block, other_ref[...]).astype(BF16)
    for j, out_ref in enumerate(out_refs):
        to = lax.bitwise_xor(col, j)
        y, x = lax.div(to, 2), lax.rem(to, 2)
        out_ref[: n * tokens] = part_ref[y, :, pl.ds(pl.multiple_of(x * HD, HD), HD)]
        for i in range(n):
            rows = pl.ds(pl.multiple_of(i * tokens + x * half, half), half)
            out_ref[pl.ds(n * tokens + i * half, half)] = part_ref[y, rows, 2 * HD : 3 * HD]


def grad_pieces(blocks, own, other, cost=WINDOW):
    rows = len(blocks) * blocks[0].shape[0]
    piece = jax.ShapeDtypeStruct((rows + rows // 2, HD), BF16)
    return pl.pallas_call(
        grad_kernel,
        out_shape=[piece] * COLS,
        scratch_shapes=[pltpu.VMEM((CORES, rows, own.shape[0]), BF16)],
        compiler_params=pltpu.CompilerParams(vmem_limit_bytes=20 * 2**20),
        cost_estimate=cost,
        name="grad_pieces",
    )(*blocks, own, other)


def group(ref, index):
    width = ref.shape[1] // CORES
    return ref[:, pl.ds(pl.multiple_of(index * width, width), width)]


def term_kernel(block_ref, own_ref, other_ref, out_ref):
    core = lax.rem(lax.axis_index("row"), CORES)
    out = jnp.dot(group(block_ref, core), own_ref[...], preferred_element_type=F32)
    out += jnp.dot(group(block_ref, 1 - core), other_ref[...], preferred_element_type=F32)
    out_ref[...] = out.astype(out_ref.dtype)


def mixed_term(block, own, other, dtype, cost=SMALL):
    return pl.pallas_call(
        term_kernel,
        out_shape=jax.ShapeDtypeStruct((block.shape[0], own.shape[1]), dtype),
        compiler_params=pltpu.CompilerParams(vmem_limit_bytes=20 * 2**20),
        cost_estimate=cost,
        name="mixed_term",
    )(block, own, other)


def weight_grad_kernel(n, *refs):
    head_refs, grad_refs, total_refs, out_ref = refs[:n], refs[n : 2 * n], refs[2 * n : -1], refs[-1]
    width = out_ref.shape[1] // 4
    for i in range(4):
        columns = pl.ds(i * width, width)
        total = sum(tn(h[...], g[:, columns]) for h, g in zip(head_refs, grad_refs))
        for total_ref in total_refs:
            total = total + total_ref[:, columns].astype(F32)
        out_ref[:, columns] = total.astype(BF16)


def weight_grad_part(heads, grads, *total):
    return pl.pallas_call(
        functools.partial(weight_grad_kernel, len(heads)),
        out_shape=jax.ShapeDtypeStruct((heads[0].shape[1], grads[0].shape[1]), BF16),
        compiler_params=pltpu.CompilerParams(vmem_limit_bytes=28 * 2**20),
        cost_estimate=WINDOW,
        name="weight_grad",
    )(*heads, *grads, *total)


def unpack_kernel(*refs):
    in_refs, out_refs = refs[:COLS], refs[COLS:]
    tokens = out_refs[0].shape[0]
    half = tokens // 2
    col = lax.axis_index("col")
    for j, in_ref in enumerate(in_refs):
        of = lax.bitwise_xor(col, j)
        y, x = lax.div(of, 2), lax.rem(of, 2)
        a = pl.ds(pl.multiple_of((3 * y + x) * HD, HD), HD)
        b = pl.ds(pl.multiple_of((3 * y + 2) * HD, HD), HD)
        out_refs[0][:, a] = in_ref[:tokens]
        out_refs[0][pl.ds(pl.multiple_of(x * half, half), half), b] = in_ref[tokens : tokens + half]
        for i in range(2):
            at = tokens + half + 2 * i * tokens
            out_refs[1 + i][:, a] = in_ref[at : at + tokens]
    for y in range(2):
        b = pl.ds((3 * y + 2) * HD, HD)
        for i in range(2):
            at = tokens + half + (2 * i + 1) * tokens

            def load(x):
                entry = lax.bitwise_xor(col, 2 * y + x)
                block = in_refs[0][at : at + tokens].astype(F32)
                for j in range(1, COLS):
                    block = jnp.where(entry == j, in_refs[j][at : at + tokens].astype(F32), block)
                return block

            out_refs[1 + i][:, b] = (load(0) + load(1)).astype(BF16)


def unpack(blocks, tokens, width):
    return pl.pallas_call(
        unpack_kernel,
        out_shape=[jax.ShapeDtypeStruct((tokens, width), BF16)] * 3,
        cost_estimate=SMALL,
        name="unpack_outputs",
    )(*blocks)


def fence_kernel(in_ref, out_ref):
    del in_ref, out_ref


def fence(*earlier):
    mark = lax.optimization_barrier((jnp.zeros((8, 128), F32), earlier))[0]
    return pl.pallas_call(
        fence_kernel,
        in_specs=[pl.BlockSpec(memory_space=pl.ANY)],
        out_specs=pl.BlockSpec(memory_space=pl.ANY),
        out_shape=jax.ShapeDtypeStruct(mark.shape, mark.dtype),
        compiler_params=pltpu.CompilerParams(has_side_effects=True),
        cost_estimate=WINDOW,
        name="fence",
    )(mark)


def after(value, *earlier):
    return lax.optimization_barrier((value, earlier))[0]


def per_device_fast(queries, keys_tile, values_tile, out_weight, out_grad):
    tokens = queries.shape[0]
    half = tokens // 2
    own = PLANES * tokens
    width = out_weight.shape[0]
    row, col = lax.axis_index("row"), lax.axis_index("col")
    plane, core = row // CORES, row % CORES

    def head(block, g):
        return block[:, g * HD : (g + 1) * HD]

    def to_col(block, j):
        return lax.ppermute(block, "col", col_xor(j))

    def to_plane(block, s):
        return lax.ppermute(block, "row", row_shift(s))

    def swap(block):
        return lax.ppermute(block, "row", SWAP)

    grad_1 = to_plane(out_grad, 1)
    grad_3 = to_plane(out_grad, -1)
    weights = (out_weight, swap(out_weight))

    pieces = pack(*after((queries, keys_tile, values_tile), fence()))
    pieces = after(pieces, weights[1])
    moved = after([to_col(pieces[j], j) for j in (1, 2, 3)], fence(pieces))
    over_col = jnp.stack([pieces[0], *moved])

    arrived = [pick(over_col, col ^ plane)]
    for s in ORDER[1:]:
        arrived.append(to_plane(pick(over_col, col ^ ((plane + s) % PLANES)), s))

    early = grad_pieces((out_grad, grad_1, grad_3), *weights)
    early = list(early)
    early[1:] = [to_col(block, j) for j, block in enumerate(after(early[1:], arrived[1:3]), 1)]

    own_part = after(arrived, early)
    other_part = [swap(block) for block in own_part]
    other_part = after(other_part, fence(own_part))

    grad_2 = to_plane(after(grad_1, arrived), 1)
    grads = [out_grad, grad_1, grad_3, grad_2]

    probs, attn, q, k, v = attention_forward(own_part, other_part, tokens)
    grad_2 = after(grad_2, attn)

    def plane_heads(rows, every):
        by_col = [pick(every, col ^ d) for d in range(COLS)]
        columns = []
        for y in range(2):
            columns += [by_col[2 * y][:rows], by_col[2 * y + 1][:rows]]
            halves = [by_col[2 * y + x][rows:].reshape(-1, half, HD) for x in range(2)]
            columns.append(jnp.concatenate(halves, axis=1).reshape(rows, HD))
        return jnp.concatenate(columns, axis=1)

    attn_a, attn_b = attn[:own], attn[own:]
    sent = jnp.concatenate([attn_a[3 * tokens :], attn_b[3 * half :]])
    got = after([to_col(sent, j) for j in (1, 2, 3)], grad_2)
    heads_2 = plane_heads(tokens, jnp.stack([sent, *got]))
    term_2 = mixed_term(heads_2, *weights, BF16)
    mixed_2 = to_plane(term_2, 1)
    late = grad_pieces((after(grad_2, term_2),), *weights)
    late = [late[0]] + [to_col(late[j], j) for j in (1, 2, 3)]
    sent = jnp.concatenate([attn_a[: 3 * tokens], attn_b[: 3 * half]])
    pair = jnp.stack([sent, to_col(sent, 1)])
    rest = [pair, to_col(pair, 2)]

    dq, dkv, dkv_other = attention_backward(q, k, v, probs, attn, early, late)
    rest, mixed_2 = after((rest, mixed_2), dq)

    dkv_other = jnp.stack([jnp.stack([swap(dkv_other[i, h]) for h in range(2)]) for i in range(2)])
    dkv = dkv + dkv_other.astype(F32)
    dkv = dkv.astype(BF16).reshape(4, PLANES, tokens, HD)
    dq_a = dq[:own].reshape(PLANES, tokens, HD)
    dq_b = dq[own:].reshape(PLANES, half, HD)
    home = [
        jnp.concatenate([dq_a[p], dq_b[p]] + [dkv[i, p] for i in range(4)])
        for p in (ORDER.index(s) for s in range(PLANES))
    ]

    away = [to_plane(home[s], -s) for s in range(1, PLANES)]

    heads_rest = plane_heads(3 * tokens, jnp.concatenate(rest))
    heads = [heads_rest[p * tokens : (p + 1) * tokens] for p in range(3)] + [heads_2]
    ours, theirs = [
        [lax.dynamic_slice_in_dim(h, g * width, width, 1) for h in heads] for g in (core, 1 - core)
    ]
    total = weight_grad_part(after(theirs, home), grads)

    head_0, head_1, head_3 = after(heads[:3], total)
    term_1 = mixed_term(head_1, *weights, BF16)
    mixed_1 = to_plane(term_1, -1)
    term_3 = (mixed_2.astype(F32) + mixed_term(head_3, *weights, F32)).astype(BF16)
    total = swap(total)
    term_0 = mixed_term(after(head_0, term_1, term_3), *weights, F32, WINDOW)

    away, total = after((away, total), term_0)
    home = [home[0], *away]
    weight_grad = weight_grad_part(after(ours, home), grads, total)

    mixed_3 = to_plane(after(term_3, home), 1)

    home = jnp.stack(home)
    back = [pick(home, (col - plane) % PLANES)] + [
        to_col(pick(home, ((col ^ j) - plane) % PLANES), j) for j in (1, 2, 3)
    ]
    query_g, key_g, value_g = unpack(after(back, weight_grad), tokens, queries.shape[1])
    mixed_3 = after(mixed_3, query_g)
    mixed_1 = after(mixed_1, weight_grad)
    mixed = (term_0 + mixed_1.astype(F32) + mixed_3.astype(F32)).astype(BF16)
    return (mixed, query_g, key_g, value_g, weight_grad)


def solution(mesh):
    spec = P("row", "col")
    fast = mesh.shape["row"] == PLANES * CORES and mesh.shape["col"] == COLS

    def run(queries, keys_tile, values_tile, out_weight, out_grad):
        heads = queries.shape[1] // HD
        fits = fast and heads == 6 * COLS and queries.shape[0] % (32 * mesh.shape["row"]) == 0
        return jax.shard_map(
            per_device_fast if fits else per_device,
            mesh=mesh,
            in_specs=(spec,) * 5,
            out_specs=(spec,) * 5,
            check_vma=False,
        )(queries, keys_tile, values_tile, out_weight, out_grad)

    return run
```

```python
import functools

import jax
import jax.numpy as jnp
from jax import lax
from jax.experimental import pallas as pl
from jax.experimental.pallas import tpu as pltpu
from jax.sharding import PartitionSpec as P

HD = 128
SCALE = HD ** (-0.5)
LOG2E = 1.4426950408889634
F32 = jnp.float32
BF16 = jnp.bfloat16


def head_forward(args):
    query_head, key_head, value_head = args
    scores = jnp.einsum(
        "qd,kd->qk", query_head, key_head, preferred_element_type=jnp.float32
    ) * HD ** (-0.5)
    top = jnp.max(scores, axis=1, keepdims=True)
    lse = top[:, 0] + jnp.log(jnp.sum(jnp.exp(scores - top), axis=1))
    probs = jnp.exp(scores - lse[:, None]).astype(jnp.bfloat16)
    attn = jnp.dot(probs, value_head, preferred_element_type=jnp.float32).astype(jnp.bfloat16)
    return (attn, lse)


def score_grads(query_head, key_head, value_head, grad_head, lse, delta):
    scores = jnp.einsum(
        "qd,kd->qk", query_head, key_head, preferred_element_type=jnp.float32
    ) * HD ** (-0.5)
    probs = jnp.exp(scores - lse[:, None]).astype(jnp.bfloat16)
    dprob = jnp.einsum("qd,kd->qk", grad_head, value_head, preferred_element_type=jnp.float32)
    dscore = (probs.astype(jnp.float32) * (dprob - delta[:, None]) * HD ** (-0.5)).astype(
        jnp.bfloat16
    )
    return (probs, dscore)


def split_heads(block):
    return block.reshape(block.shape[0], block.shape[1] // HD, HD).transpose(1, 0, 2)


def merge_heads(block):
    return block.transpose(1, 0, 2).reshape(block.shape[1], block.shape[0] * HD)


def per_device(queries, keys_tile, values_tile, out_weight, out_grad):
    query3 = split_heads(queries)
    key_local = split_heads(keys_tile)
    value_local = split_heads(values_tile)
    key_every, value_every = (
        lax.all_gather(key_local, "row", axis=1, tiled=True),
        lax.all_gather(value_local, "row", axis=1, tiled=True),
    )
    attn3, lse = lax.map(head_forward, (query3, key_every, value_every))
    attn = merge_heads(attn3)
    attn_row = lax.all_gather(attn, "col", axis=1, tiled=True)
    weight_col = lax.all_gather(out_weight, "row", axis=0, tiled=True)
    mixed = jnp.dot(attn_row, weight_col, preferred_element_type=jnp.float32).astype(jnp.bfloat16)
    partial_grad = jnp.einsum("rc,fc->rf", out_grad, weight_col, preferred_element_type=jnp.float32)
    d_attn = lax.psum_scatter(partial_grad, "col", scatter_dimension=1, tiled=True).astype(
        jnp.bfloat16
    )
    weight_grad = lax.psum_scatter(
        jnp.einsum("rf,rc->fc", attn_row, out_grad, preferred_element_type=jnp.float32).astype(
            jnp.bfloat16
        ),
        "row",
        scatter_dimension=0,
        tiled=True,
    )
    grad3 = split_heads(d_attn)
    delta = jnp.sum(grad3.astype(jnp.float32) * attn3.astype(jnp.float32), axis=2)

    def head_backward(args):
        query_head, key_head, value_head, grad_head, lse_head, delta_head = args
        probs, dscore = score_grads(
            query_head, key_head, value_head, grad_head, lse_head, delta_head
        )
        query_g = jnp.dot(dscore, key_head, preferred_element_type=jnp.float32).astype(jnp.bfloat16)
        key_term = jnp.einsum("qk,qd->kd", dscore, query_head, preferred_element_type=jnp.float32)
        value_term = jnp.einsum("qk,qd->kd", probs, grad_head, preferred_element_type=jnp.float32)
        return (query_g, key_term, value_term)

    query_g3, key_terms, value_terms = lax.map(
        head_backward, (query3, key_every, value_every, grad3, lse, delta)
    )
    key_g3, value_g3 = (
        lax.psum_scatter(key_terms, "row", scatter_dimension=1, tiled=True),
        lax.psum_scatter(value_terms, "row", scatter_dimension=1, tiled=True),
    )
    key_g3 = key_g3.astype(jnp.bfloat16)
    value_g3 = value_g3.astype(jnp.bfloat16)
    return (mixed, merge_heads(query_g3), merge_heads(key_g3), merge_heads(value_g3), weight_grad)


PLANES, CORES, COLS = 4, 2, 4
ORDER = (0, 1, 3, 2)
WINDOW = pl.CostEstimate(flops=4 * 10**10, bytes_accessed=0, transcendentals=0)
SMALL = pl.CostEstimate(flops=10**6, bytes_accessed=10**3, transcendentals=0)


def row_shift(s):
    return [
        (CORES * z + k, CORES * ((z + s) % PLANES) + k)
        for z in range(PLANES)
        for k in range(CORES)
    ]


SWAP = [(CORES * z + k, CORES * z + 1 - k) for z in range(PLANES) for k in range(CORES)]


def col_xor(j):
    return [(c, c ^ j) for c in range(COLS)]


def pick(stack, index):
    return lax.dynamic_index_in_dim(stack, index, 0, keepdims=False)


def nt(a, b):
    return lax.dot_general(a, b, (((1,), (1,)), ((), ())), preferred_element_type=F32)


def tn(a, b):
    return lax.dot_general(a, b, (((0,), (0,)), ((), ())), preferred_element_type=F32)


def forward_kernel(*refs):
    own_refs, other_refs, (p_ref, attn_ref, q_ref, k_ref, v_ref) = refs[:PLANES], refs[PLANES:-5], refs[-5:]
    step = pl.program_id(0)
    rows = attn_ref.shape[0]

    @pl.when(step == 0)
    def _():
        tokens = k_ref.shape[1] // (2 * PLANES)
        half = tokens // 2
        for p, own_ref in enumerate(own_refs):
            q_ref[p * tokens : (p + 1) * tokens] = own_ref[:tokens]
            at = PLANES * tokens + p * half
            q_ref[at : at + half] = own_ref[tokens : tokens + half]
        for p, in_ref in enumerate(own_refs + other_refs):
            for i in range(4):
                at = tokens + half + i * tokens
                out_ref = (k_ref, v_ref)[i // 2]
                out_ref[i % 2, p * tokens : (p + 1) * tokens] = in_ref[at : at + tokens]

    head = lax.div(step, 2)
    raw = nt(k_ref[head], q_ref[pl.ds(pl.multiple_of(step * rows, rows), rows)])
    top = jnp.max(raw, axis=0, keepdims=True)
    e = jnp.exp2((raw - top) * (SCALE * LOG2E))
    total = jnp.sum(e, axis=0, keepdims=True)
    probs = (e * (1.0 / total)).astype(BF16)
    p_ref[0] = probs
    attn_ref[...] = tn(v_ref[head], probs).T.astype(BF16)


def attention_forward(own, other, tokens):
    rows, keys = 2 * tokens, 2 * PLANES * tokens

    def whole(*shape):
        return pl.BlockSpec(shape, lambda i: (0,) * len(shape))

    return pl.pallas_call(
        forward_kernel,
        grid=(3,),
        in_specs=[whole(*own[0].shape)] * (2 * PLANES),
        out_specs=[
            pl.BlockSpec((1, keys, rows), lambda i: (i, 0, 0)),
            pl.BlockSpec((rows, HD), lambda i: (i, 0)),
            whole(3 * rows, HD),
            whole(2, keys, HD),
            whole(2, keys, HD),
        ],
        out_shape=[
            pltpu.HBM((3, keys, rows), BF16),
            jax.ShapeDtypeStruct((3 * rows, HD), BF16),
            jax.ShapeDtypeStruct((3 * rows, HD), BF16),
            jax.ShapeDtypeStruct((2, keys, HD), BF16),
            jax.ShapeDtypeStruct((2, keys, HD), BF16),
        ],
        compiler_params=pltpu.CompilerParams(vmem_limit_bytes=24 * 2**20),
        cost_estimate=WINDOW,
        name="attention_forward",
    )(*own, *other)


def backward_kernel(
    q_ref, k_ref, v_ref, p_ref, attn_ref, *refs
):
    early_refs, late_refs, refs = refs[:1], refs[1 : 1 + COLS], refs[1 + COLS :]
    dq_ref, own_ref, other_ref, grad_ref, sums_ref = refs
    step = pl.program_id(0)
    rows = q_ref.shape[0]

    @pl.when(step == 0)
    def _():
        early_a, late_a = early_refs[0].shape[0] * 2 // 3, late_refs[0].shape[0] * 2 // 3
        early = early_refs[0][...]
        late = sum(ref[...].astype(F32) for ref in late_refs).astype(BF16)
        own = early_a + late_a
        grad_ref[:early_a] = early[:early_a]
        grad_ref[early_a:own] = late[:late_a]
        grad_ref[own : own + early_a // 2] = early[early_a:]
        grad_ref[own + early_a // 2 :] = late[late_a:]

    grad = grad_ref[pl.ds(pl.multiple_of(step * rows, rows), rows)]
    product = grad.astype(F32) * attn_ref[...].astype(F32)
    delta = jnp.sum(product.T, axis=0, keepdims=True)
    probs = p_ref[0]
    dprob = nt(v_ref[0], grad)
    dscore = (probs.astype(F32) * (dprob - delta) * SCALE).astype(BF16)
    dq_ref[...] = tn(k_ref[0], dscore).T.astype(BF16)
    dk = jnp.dot(dscore, q_ref[...], preferred_element_type=F32)
    dv = jnp.dot(probs, grad, preferred_element_type=F32)

    @pl.when(step == 0)
    def _():
        sums_ref[0] = dk
        sums_ref[1] = dv

    @pl.when(step != 0)
    def _():
        half = dk.shape[0] // 2
        for i, new in enumerate((dk, dv)):
            new = jnp.where(step == 1, sums_ref[i], 0.0) + new
            own_ref[i, 0] = new[:half]
            other_ref[i, 0] = new[half:].astype(BF16)


def attention_backward(q, k, v, probs, attn, early, late):
    rows, keys = q.shape[0] // 3, k.shape[1]
    by_query = pl.BlockSpec((rows, HD), lambda i: (i, 0))
    by_head = pl.BlockSpec((1, keys, HD), lambda i: (i // 2, 0, 0))
    by_half = pl.BlockSpec((2, 1, keys // 2, HD), lambda i: (0, i // 2, 0, 0))
    return pl.pallas_call(
        backward_kernel,
        grid=(3,),
        in_specs=[
            by_query,
            by_head,
            by_head,
            pl.BlockSpec((1, keys, rows), lambda i: (i, 0, 0)),
            by_query,
            *[pl.BlockSpec(block.shape, lambda i: (0, 0)) for block in (*early, *late)],
        ],
        out_specs=[by_query, by_half, by_half],
        out_shape=[
            jax.ShapeDtypeStruct(q.shape, BF16),
            jax.ShapeDtypeStruct((2, 2, keys // 2, HD), F32),
            jax.ShapeDtypeStruct((2, 2, keys // 2, HD), BF16),
        ],
        scratch_shapes=[pltpu.VMEM(q.shape, BF16), pltpu.VMEM((2, keys, HD), F32)],
        compiler_params=pltpu.CompilerParams(vmem_limit_bytes=20 * 2**20),
        cost_estimate=WINDOW,
        name="attention_backward",
    )(q, k, v, probs, attn, *early, *late)


def pack_kernel(q_ref, k_ref, v_ref, *out_refs):
    tokens = q_ref.shape[0]
    half = tokens // 2
    col = lax.axis_index("col")
    for j, out_ref in enumerate(out_refs):
        to = lax.bitwise_xor(col, j)
        y, x = lax.div(to, 2), lax.rem(to, 2)
        a = pl.ds(pl.multiple_of((3 * y + x) * HD, HD), HD)
        b = pl.ds(pl.multiple_of((3 * y + 2) * HD, HD), HD)
        at = tokens + half
        out_ref[:tokens] = q_ref[:, a]
        out_ref[tokens:at] = q_ref[pl.ds(pl.multiple_of(x * half, half), half), b]
        for i, block in enumerate((k_ref[:, a], k_ref[:, b], v_ref[:, a], v_ref[:, b])):
            out_ref[at + i * tokens : at + (i + 1) * tokens] = block


def pack(queries, keys, values):
    tokens = queries.shape[0]
    piece = jax.ShapeDtypeStruct((tokens // 2 + 5 * tokens, HD), BF16)
    return pl.pallas_call(
        pack_kernel,
        out_shape=[piece] * COLS,
        cost_estimate=WINDOW,
        name="pack_inputs",
    )(queries, keys, values)


def grad_kernel(*refs):
    n = len(refs) - 2 - COLS - 1
    own_ref, other_ref = refs[n : n + 2]
    out_refs, part_ref = refs[n + 2 : -1], refs[-1]
    tokens = refs[0].shape[0]
    half = tokens // 2
    core, col = lax.rem(lax.axis_index("row"), CORES), lax.axis_index("col")
    for i in range(n):
        rows = pl.ds(i * tokens, tokens)
        block = refs[i][...]
        part_ref[core, rows] = nt(block, own_ref[...]).astype(BF16)
        part_ref[1 - core, rows] = nt(block, other_ref[...]).astype(BF16)
    for j, out_ref in enumerate(out_refs):
        to = lax.bitwise_xor(col, j)
        y, x = lax.div(to, 2), lax.rem(to, 2)
        out_ref[: n * tokens] = part_ref[y, :, pl.ds(pl.multiple_of(x * HD, HD), HD)]
        for i in range(n):
            rows = pl.ds(pl.multiple_of(i * tokens + x * half, half), half)
            out_ref[pl.ds(n * tokens + i * half, half)] = part_ref[y, rows, 2 * HD : 3 * HD]


def grad_pieces(blocks, own, other, cost=WINDOW):
    rows = len(blocks) * blocks[0].shape[0]
    piece = jax.ShapeDtypeStruct((rows + rows // 2, HD), BF16)
    return pl.pallas_call(
        grad_kernel,
        out_shape=[piece] * COLS,
        scratch_shapes=[pltpu.VMEM((CORES, rows, own.shape[0]), BF16)],
        compiler_params=pltpu.CompilerParams(vmem_limit_bytes=20 * 2**20),
        cost_estimate=cost,
        name="grad_pieces",
    )(*blocks, own, other)


def group(ref, index):
    width = ref.shape[1] // CORES
    return ref[:, pl.ds(pl.multiple_of(index * width, width), width)]


def term_kernel(block_ref, own_ref, other_ref, out_ref):
    core = lax.rem(lax.axis_index("row"), CORES)
    out = jnp.dot(group(block_ref, core), own_ref[...], preferred_element_type=F32)
    out += jnp.dot(group(block_ref, 1 - core), other_ref[...], preferred_element_type=F32)
    out_ref[...] = out.astype(out_ref.dtype)


def mixed_term(block, own, other, dtype, cost=SMALL):
    return pl.pallas_call(
        term_kernel,
        out_shape=jax.ShapeDtypeStruct((block.shape[0], own.shape[1]), dtype),
        compiler_params=pltpu.CompilerParams(vmem_limit_bytes=20 * 2**20),
        cost_estimate=cost,
        name="mixed_term",
    )(block, own, other)


def weight_grad_kernel(n, *refs):
    head_refs, grad_refs, total_refs, out_ref = refs[:n], refs[n : 2 * n], refs[2 * n : -1], refs[-1]
    width = out_ref.shape[1] // 4
    for i in range(4):
        columns = pl.ds(i * width, width)
        total = sum(tn(h[...], g[:, columns]) for h, g in zip(head_refs, grad_refs))
        for total_ref in total_refs:
            total = total + total_ref[:, columns].astype(F32)
        out_ref[:, columns] = total.astype(BF16)


def weight_grad_part(heads, grads, *total):
    return pl.pallas_call(
        functools.partial(weight_grad_kernel, len(heads)),
        out_shape=jax.ShapeDtypeStruct((heads[0].shape[1], grads[0].shape[1]), BF16),
        compiler_params=pltpu.CompilerParams(vmem_limit_bytes=28 * 2**20),
        cost_estimate=WINDOW,
        name="weight_grad",
    )(*heads, *grads, *total)


def unpack_kernel(*refs):
    in_refs, out_refs = refs[:COLS], refs[COLS:]
    tokens = out_refs[0].shape[0]
    half = tokens // 2
    col = lax.axis_index("col")
    for j, in_ref in enumerate(in_refs):
        of = lax.bitwise_xor(col, j)
        y, x = lax.div(of, 2), lax.rem(of, 2)
        a = pl.ds(pl.multiple_of((3 * y + x) * HD, HD), HD)
        b = pl.ds(pl.multiple_of((3 * y + 2) * HD, HD), HD)
        out_refs[0][:, a] = in_ref[:tokens]
        out_refs[0][pl.ds(pl.multiple_of(x * half, half), half), b] = in_ref[tokens : tokens + half]
        for i in range(2):
            at = tokens + half + 2 * i * tokens
            out_refs[1 + i][:, a] = in_ref[at : at + tokens]
    for y in range(2):
        b = pl.ds((3 * y + 2) * HD, HD)
        for i in range(2):
            at = tokens + half + (2 * i + 1) * tokens

            def load(x):
                entry = lax.bitwise_xor(col, 2 * y + x)
                block = in_refs[0][at : at + tokens].astype(F32)
                for j in range(1, COLS):
                    block = jnp.where(entry == j, in_refs[j][at : at + tokens].astype(F32), block)
                return block

            out_refs[1 + i][:, b] = (load(0) + load(1)).astype(BF16)


def unpack(blocks, tokens, width):
    return pl.pallas_call(
        unpack_kernel,
        out_shape=[jax.ShapeDtypeStruct((tokens, width), BF16)] * 3,
        cost_estimate=SMALL,
        name="unpack_outputs",
    )(*blocks)


def fence_kernel(in_ref, out_ref):
    del in_ref, out_ref


def fence(*earlier):
    mark = lax.optimization_barrier((jnp.zeros((8, 128), F32), earlier))[0]
    return pl.pallas_call(
        fence_kernel,
        in_specs=[pl.BlockSpec(memory_space=pl.ANY)],
        out_specs=pl.BlockSpec(memory_space=pl.ANY),
        out_shape=jax.ShapeDtypeStruct(mark.shape, mark.dtype),
        compiler_params=pltpu.CompilerParams(has_side_effects=True),
        cost_estimate=WINDOW,
        name="fence",
    )(mark)


def fence0(mark):
    return pl.pallas_call(
        fence_kernel,
        in_specs=[pl.BlockSpec(memory_space=pl.ANY)],
        out_specs=pl.BlockSpec(memory_space=pl.ANY),
        out_shape=jax.ShapeDtypeStruct((8, 128), F32),
        compiler_params=pltpu.CompilerParams(has_side_effects=True),
        cost_estimate=WINDOW,
        name="fence",
    )(mark)


def after(value, *earlier):
    return lax.optimization_barrier((value, earlier))[0]


def per_device_fast(queries, keys_tile, values_tile, out_weight, out_grad):
    tokens = queries.shape[0]
    half = tokens // 2
    own = PLANES * tokens
    width = out_weight.shape[0]
    row, col = lax.axis_index("row"), lax.axis_index("col")
    plane, core = row // CORES, row % CORES

    def head(block, g):
        return block[:, g * HD : (g + 1) * HD]

    def to_col(block, j):
        return lax.ppermute(block, "col", col_xor(j))

    def to_plane(block, s):
        return lax.ppermute(block, "row", row_shift(s))

    def swap(block):
        return lax.ppermute(block, "row", SWAP)

    grad_1 = to_plane(out_grad, 1)
    grad_3 = to_plane(out_grad, -1)
    weights = (out_weight, swap(out_weight))

    pieces = pack(*after((queries, keys_tile, values_tile), fence0(queries)))
    pieces = after(pieces, weights[1])
    moved = after([to_col(pieces[j], j) for j in (1, 2, 3)], fence(pieces))
    over_col = jnp.stack([pieces[0], *moved])

    arrived = [pick(over_col, col ^ plane)]
    for s in ORDER[1:]:
        arrived.append(to_plane(pick(over_col, col ^ ((plane + s) % PLANES)), s))

    early = grad_pieces((out_grad, grad_1, grad_3), *weights)
    early = list(early)
    early[1:] = [to_col(block, j) for j, block in enumerate(after(early[1:], arrived[1:3]), 1)]

    own_part = after(arrived, early)
    other_part = [swap(block) for block in own_part]
    other_part = after(other_part, fence(own_part))

    grad_2 = to_plane(after(grad_1, arrived), 1)
    grads = [out_grad, grad_1, grad_3, grad_2]

    probs, attn, q, k, v = attention_forward(own_part, other_part, tokens)
    grad_2 = after(grad_2, attn)
    early = [sum(t.astype(F32) for t in after(early, attn)).astype(BF16)]

    def plane_heads(rows, every):
        by_col = [pick(every, col ^ d) for d in range(COLS)]
        columns = []
        for y in range(2):
            columns += [by_col[2 * y][:rows], by_col[2 * y + 1][:rows]]
            halves = [by_col[2 * y + x][rows:].reshape(-1, half, HD) for x in range(2)]
            columns.append(jnp.concatenate(halves, axis=1).reshape(rows, HD))
        return jnp.concatenate(columns, axis=1)

    attn_a, attn_b = attn[:own], attn[own:]
    sent = jnp.concatenate([attn_a[3 * tokens :], attn_b[3 * half :]])
    late = grad_pieces((grad_2,), *weights)
    got = after([to_col(sent, j) for j in (1, 2, 3)], late)
    heads_2 = plane_heads(tokens, jnp.stack([sent, *got]))
    term_2 = mixed_term(heads_2, *weights, BF16)
    mixed_2 = to_plane(term_2, 1)
    late = [late[0]] + [to_col(late[j], j) for j in (1, 2, 3)]
    sent = jnp.concatenate([attn_a[: 3 * tokens], attn_b[: 3 * half]])
    pair = jnp.stack([sent, to_col(sent, 1)])
    rest = [pair, to_col(pair, 2)]

    dq, dkv, dkv_other = attention_backward(q, k, v, probs, attn, early, late)
    rest, mixed_2 = after((rest, mixed_2), dq)

    dkv_other = jnp.stack([jnp.stack([swap(dkv_other[i, h]) for h in range(2)]) for i in range(2)])
    dkv = dkv + dkv_other.astype(F32)
    dkv = dkv.astype(BF16).reshape(4, PLANES, tokens, HD)
    dq_a = dq[:own].reshape(PLANES, tokens, HD)
    dq_b = dq[own:].reshape(PLANES, half, HD)
    home = [
        jnp.concatenate([dq_a[p], dq_b[p]] + [dkv[i, p] for i in range(4)])
        for p in (ORDER.index(s) for s in range(PLANES))
    ]

    away = [to_plane(home[s], -s) for s in range(1, PLANES)]

    heads_rest = plane_heads(3 * tokens, jnp.concatenate(rest))
    heads = [heads_rest[p * tokens : (p + 1) * tokens] for p in range(3)] + [heads_2]
    ours, theirs = [
        [lax.dynamic_slice_in_dim(h, g * width, width, 1) for h in heads] for g in (core, 1 - core)
    ]
    total = weight_grad_part(after(theirs, home), grads)

    head_0, head_1, head_3 = after(heads[:3], total)
    term_1 = mixed_term(head_1, *weights, BF16)
    term_3 = (mixed_2.astype(F32) + mixed_term(head_3, *weights, F32)).astype(BF16)
    total = swap(total)
    term_0 = mixed_term(after(head_0, term_1, term_3), *weights, F32, WINDOW)

    away, total = after((away, total), term_0)
    home = [home[0], *away]
    weight_grad = weight_grad_part(after(ours, home), grads, total)

    mixed_1 = to_plane(after(term_1, home), -1)
    mixed_3 = to_plane(after(term_3, home), 1)

    home = after(jnp.stack(home), weight_grad)
    back = [pick(home, (col - plane) % PLANES)] + [
        to_col(pick(home, ((col ^ j) - plane) % PLANES), j) for j in (1, 2, 3)
    ]
    query_g, key_g, value_g = unpack(back, tokens, queries.shape[1])
    mixed_1, mixed_3 = after((mixed_1, mixed_3), query_g)
    mixed = (term_0 + mixed_1.astype(F32) + mixed_3.astype(F32)).astype(BF16)
    return (mixed, query_g, key_g, value_g, weight_grad)


def solution(mesh):
    spec = P("row", "col")
    fast = mesh.shape["row"] == PLANES * CORES and mesh.shape["col"] == COLS

    def run(queries, keys_tile, values_tile, out_weight, out_grad):
        heads = queries.shape[1] // HD
        fits = fast and heads == 6 * COLS and queries.shape[0] % (32 * mesh.shape["row"]) == 0
        return jax.shard_map(
            per_device_fast if fits else per_device,
            mesh=mesh,
            in_specs=(spec,) * 5,
            out_specs=(spec,) * 5,
            check_vma=False,
        )(queries, keys_tile, values_tile, out_weight, out_grad)

    return run
```

```python
import functools

import jax
import jax.numpy as jnp
from jax import lax
from jax.experimental import pallas as pl
from jax.experimental.pallas import tpu as pltpu
from jax.sharding import PartitionSpec as P

HD = 128
SCALE = HD ** (-0.5)
LOG2E = 1.4426950408889634
F32 = jnp.float32
BF16 = jnp.bfloat16


def head_forward(args):
    query_head, key_head, value_head = args
    scores = jnp.einsum(
        "qd,kd->qk", query_head, key_head, preferred_element_type=jnp.float32
    ) * HD ** (-0.5)
    top = jnp.max(scores, axis=1, keepdims=True)
    lse = top[:, 0] + jnp.log(jnp.sum(jnp.exp(scores - top), axis=1))
    probs = jnp.exp(scores - lse[:, None]).astype(jnp.bfloat16)
    attn = jnp.dot(probs, value_head, preferred_element_type=jnp.float32).astype(jnp.bfloat16)
    return (attn, lse)


def score_grads(query_head, key_head, value_head, grad_head, lse, delta):
    scores = jnp.einsum(
        "qd,kd->qk", query_head, key_head, preferred_element_type=jnp.float32
    ) * HD ** (-0.5)
    probs = jnp.exp(scores - lse[:, None]).astype(jnp.bfloat16)
    dprob = jnp.einsum("qd,kd->qk", grad_head, value_head, preferred_element_type=jnp.float32)
    dscore = (probs.astype(jnp.float32) * (dprob - delta[:, None]) * HD ** (-0.5)).astype(
        jnp.bfloat16
    )
    return (probs, dscore)


def split_heads(block):
    return block.reshape(block.shape[0], block.shape[1] // HD, HD).transpose(1, 0, 2)


def merge_heads(block):
    return block.transpose(1, 0, 2).reshape(block.shape[1], block.shape[0] * HD)


def per_device(queries, keys_tile, values_tile, out_weight, out_grad):
    query3 = split_heads(queries)
    key_local = split_heads(keys_tile)
    value_local = split_heads(values_tile)
    key_every, value_every = (
        lax.all_gather(key_local, "row", axis=1, tiled=True),
        lax.all_gather(value_local, "row", axis=1, tiled=True),
    )
    attn3, lse = lax.map(head_forward, (query3, key_every, value_every))
    attn = merge_heads(attn3)
    attn_row = lax.all_gather(attn, "col", axis=1, tiled=True)
    weight_col = lax.all_gather(out_weight, "row", axis=0, tiled=True)
    mixed = jnp.dot(attn_row, weight_col, preferred_element_type=jnp.float32).astype(jnp.bfloat16)
    partial_grad = jnp.einsum("rc,fc->rf", out_grad, weight_col, preferred_element_type=jnp.float32)
    d_attn = lax.psum_scatter(partial_grad, "col", scatter_dimension=1, tiled=True).astype(
        jnp.bfloat16
    )
    weight_grad = lax.psum_scatter(
        jnp.einsum("rf,rc->fc", attn_row, out_grad, preferred_element_type=jnp.float32).astype(
            jnp.bfloat16
        ),
        "row",
        scatter_dimension=0,
        tiled=True,
    )
    grad3 = split_heads(d_attn)
    delta = jnp.sum(grad3.astype(jnp.float32) * attn3.astype(jnp.float32), axis=2)

    def head_backward(args):
        query_head, key_head, value_head, grad_head, lse_head, delta_head = args
        probs, dscore = score_grads(
            query_head, key_head, value_head, grad_head, lse_head, delta_head
        )
        query_g = jnp.dot(dscore, key_head, preferred_element_type=jnp.float32).astype(jnp.bfloat16)
        key_term = jnp.einsum("qk,qd->kd", dscore, query_head, preferred_element_type=jnp.float32)
        value_term = jnp.einsum("qk,qd->kd", probs, grad_head, preferred_element_type=jnp.float32)
        return (query_g, key_term, value_term)

    query_g3, key_terms, value_terms = lax.map(
        head_backward, (query3, key_every, value_every, grad3, lse, delta)
    )
    key_g3, value_g3 = (
        lax.psum_scatter(key_terms, "row", scatter_dimension=1, tiled=True),
        lax.psum_scatter(value_terms, "row", scatter_dimension=1, tiled=True),
    )
    key_g3 = key_g3.astype(jnp.bfloat16)
    value_g3 = value_g3.astype(jnp.bfloat16)
    return (mixed, merge_heads(query_g3), merge_heads(key_g3), merge_heads(value_g3), weight_grad)


PLANES, CORES, COLS = 4, 2, 4
ORDER = (0, 1, 3, 2)
WINDOW = pl.CostEstimate(flops=4 * 10**10, bytes_accessed=0, transcendentals=0)
SMALL = pl.CostEstimate(flops=10**6, bytes_accessed=10**3, transcendentals=0)


def row_shift(s):
    return [
        (CORES * z + k, CORES * ((z + s) % PLANES) + k)
        for z in range(PLANES)
        for k in range(CORES)
    ]


SWAP = [(CORES * z + k, CORES * z + 1 - k) for z in range(PLANES) for k in range(CORES)]


def col_xor(j):
    return [(c, c ^ j) for c in range(COLS)]


def pick(stack, index):
    return lax.dynamic_index_in_dim(stack, index, 0, keepdims=False)


def nt(a, b):
    return lax.dot_general(a, b, (((1,), (1,)), ((), ())), preferred_element_type=F32)


def tn(a, b):
    return lax.dot_general(a, b, (((0,), (0,)), ((), ())), preferred_element_type=F32)


def forward_kernel(*refs):
    own_refs, other_refs, (p_ref, attn_ref, q_ref, k_ref, v_ref) = refs[:PLANES], refs[PLANES:-5], refs[-5:]
    step = pl.program_id(0)
    rows = attn_ref.shape[0]

    @pl.when(step == 0)
    def _():
        tokens = k_ref.shape[1] // (2 * PLANES)
        half = tokens // 2
        for p, own_ref in enumerate(own_refs):
            q_ref[p * tokens : (p + 1) * tokens] = own_ref[:tokens]
            at = PLANES * tokens + p * half
            q_ref[at : at + half] = own_ref[tokens : tokens + half]
        for p, in_ref in enumerate(own_refs + other_refs):
            for i in range(4):
                at = tokens + half + i * tokens
                out_ref = (k_ref, v_ref)[i // 2]
                out_ref[i % 2, p * tokens : (p + 1) * tokens] = in_ref[at : at + tokens]

    head = lax.div(step, 2)
    raw = nt(k_ref[head], q_ref[pl.ds(pl.multiple_of(step * rows, rows), rows)])
    top = jnp.max(raw, axis=0, keepdims=True)
    e = jnp.exp2((raw - top) * (SCALE * LOG2E))
    total = jnp.sum(e, axis=0, keepdims=True)
    probs = (e * (1.0 / total)).astype(BF16)
    p_ref[0] = probs
    attn_ref[...] = tn(v_ref[head], probs).T.astype(BF16)


def attention_forward(own, other, tokens):
    rows, keys = 2 * tokens, 2 * PLANES * tokens

    def whole(*shape):
        return pl.BlockSpec(shape, lambda i: (0,) * len(shape))

    return pl.pallas_call(
        forward_kernel,
        grid=(3,),
        in_specs=[whole(*own[0].shape)] * (2 * PLANES),
        out_specs=[
            pl.BlockSpec((1, keys, rows), lambda i: (i, 0, 0)),
            pl.BlockSpec((rows, HD), lambda i: (i, 0)),
            whole(3 * rows, HD),
            whole(2, keys, HD),
            whole(2, keys, HD),
        ],
        out_shape=[
            pltpu.HBM((3, keys, rows), BF16),
            jax.ShapeDtypeStruct((3 * rows, HD), BF16),
            jax.ShapeDtypeStruct((3 * rows, HD), BF16),
            jax.ShapeDtypeStruct((2, keys, HD), BF16),
            jax.ShapeDtypeStruct((2, keys, HD), BF16),
        ],
        compiler_params=pltpu.CompilerParams(vmem_limit_bytes=24 * 2**20),
        cost_estimate=WINDOW,
        name="attention_forward",
    )(*own, *other)


def backward_kernel(
    q_ref, k_ref, v_ref, p_ref, attn_ref, *refs
):
    early_refs, late_refs, refs = refs[:1], refs[1 : 1 + COLS], refs[1 + COLS :]
    dq_ref, own_ref, other_ref, grad_ref, sums_ref = refs
    step = pl.program_id(0)
    rows = q_ref.shape[0]

    @pl.when(step == 0)
    def _():
        early_a, late_a = early_refs[0].shape[0] * 2 // 3, late_refs[0].shape[0] * 2 // 3
        early = early_refs[0][...]
        late = sum(ref[...].astype(F32) for ref in late_refs).astype(BF16)
        own = early_a + late_a
        grad_ref[:early_a] = early[:early_a]
        grad_ref[early_a:own] = late[:late_a]
        grad_ref[own : own + early_a // 2] = early[early_a:]
        grad_ref[own + early_a // 2 :] = late[late_a:]

    grad = grad_ref[pl.ds(pl.multiple_of(step * rows, rows), rows)]
    product = grad.astype(F32) * attn_ref[...].astype(F32)
    delta = jnp.sum(product.T, axis=0, keepdims=True)
    probs = p_ref[0]
    dprob = nt(v_ref[0], grad)
    dscore = (probs.astype(F32) * (dprob - delta) * SCALE).astype(BF16)
    dq_ref[...] = tn(k_ref[0], dscore).T.astype(BF16)
    dk = jnp.dot(dscore, q_ref[...], preferred_element_type=F32)
    dv = jnp.dot(probs, grad, preferred_element_type=F32)

    @pl.when(step == 0)
    def _():
        sums_ref[0] = dk
        sums_ref[1] = dv

    @pl.when(step != 0)
    def _():
        half = dk.shape[0] // 2
        for i, new in enumerate((dk, dv)):
            new = jnp.where(step == 1, sums_ref[i], 0.0) + new
            own_ref[i, 0] = new[:half]
            other_ref[i, 0] = new[half:].astype(BF16)


def attention_backward(q, k, v, probs, attn, early, late):
    rows, keys = q.shape[0] // 3, k.shape[1]
    by_query = pl.BlockSpec((rows, HD), lambda i: (i, 0))
    by_head = pl.BlockSpec((1, keys, HD), lambda i: (i // 2, 0, 0))
    by_half = pl.BlockSpec((2, 1, keys // 2, HD), lambda i: (0, i // 2, 0, 0))
    return pl.pallas_call(
        backward_kernel,
        grid=(3,),
        in_specs=[
            by_query,
            by_head,
            by_head,
            pl.BlockSpec((1, keys, rows), lambda i: (i, 0, 0)),
            by_query,
            *[pl.BlockSpec(block.shape, lambda i: (0, 0)) for block in (*early, *late)],
        ],
        out_specs=[by_query, by_half, by_half],
        out_shape=[
            jax.ShapeDtypeStruct(q.shape, BF16),
            jax.ShapeDtypeStruct((2, 2, keys // 2, HD), F32),
            jax.ShapeDtypeStruct((2, 2, keys // 2, HD), BF16),
        ],
        scratch_shapes=[pltpu.VMEM(q.shape, BF16), pltpu.VMEM((2, keys, HD), F32)],
        compiler_params=pltpu.CompilerParams(vmem_limit_bytes=20 * 2**20),
        cost_estimate=WINDOW,
        name="attention_backward",
    )(q, k, v, probs, attn, *early, *late)


def pack_kernel(q_ref, k_ref, v_ref, *out_refs):
    tokens = q_ref.shape[0]
    half = tokens // 2
    col = lax.axis_index("col")
    for j, out_ref in enumerate(out_refs):
        to = lax.bitwise_xor(col, j)
        y, x = lax.div(to, 2), lax.rem(to, 2)
        a = pl.ds(pl.multiple_of((3 * y + x) * HD, HD), HD)
        b = pl.ds(pl.multiple_of((3 * y + 2) * HD, HD), HD)
        at = tokens + half
        out_ref[:tokens] = q_ref[:, a]
        out_ref[tokens:at] = q_ref[pl.ds(pl.multiple_of(x * half, half), half), b]
        for i, block in enumerate((k_ref[:, a], k_ref[:, b], v_ref[:, a], v_ref[:, b])):
            out_ref[at + i * tokens : at + (i + 1) * tokens] = block


def pack(queries, keys, values):
    tokens = queries.shape[0]
    piece = jax.ShapeDtypeStruct((tokens // 2 + 5 * tokens, HD), BF16)
    return pl.pallas_call(
        pack_kernel,
        out_shape=[piece] * COLS,
        cost_estimate=WINDOW,
        name="pack_inputs",
    )(queries, keys, values)


def grad_kernel(*refs):
    n = len(refs) - 2 - COLS - 1
    own_ref, other_ref = refs[n : n + 2]
    out_refs, part_ref = refs[n + 2 : -1], refs[-1]
    tokens = refs[0].shape[0]
    half = tokens // 2
    core, col = lax.rem(lax.axis_index("row"), CORES), lax.axis_index("col")
    for i in range(n):
        rows = pl.ds(i * tokens, tokens)
        block = refs[i][...]
        part_ref[core, rows] = nt(block, own_ref[...]).astype(BF16)
        part_ref[1 - core, rows] = nt(block, other_ref[...]).astype(BF16)
    for j, out_ref in enumerate(out_refs):
        to = lax.bitwise_xor(col, j)
        y, x = lax.div(to, 2), lax.rem(to, 2)
        out_ref[: n * tokens] = part_ref[y, :, pl.ds(pl.multiple_of(x * HD, HD), HD)]
        for i in range(n):
            rows = pl.ds(pl.multiple_of(i * tokens + x * half, half), half)
            out_ref[pl.ds(n * tokens + i * half, half)] = part_ref[y, rows, 2 * HD : 3 * HD]


def grad_pieces(blocks, own, other, cost=WINDOW):
    rows = len(blocks) * blocks[0].shape[0]
    piece = jax.ShapeDtypeStruct((rows + rows // 2, HD), BF16)
    return pl.pallas_call(
        grad_kernel,
        out_shape=[piece] * COLS,
        scratch_shapes=[pltpu.VMEM((CORES, rows, own.shape[0]), BF16)],
        compiler_params=pltpu.CompilerParams(vmem_limit_bytes=20 * 2**20),
        cost_estimate=cost,
        name="grad_pieces",
    )(*blocks, own, other)


def group(ref, index):
    width = ref.shape[1] // CORES
    return ref[:, pl.ds(pl.multiple_of(index * width, width), width)]


def term_kernel(block_ref, own_ref, other_ref, out_ref):
    core = lax.rem(lax.axis_index("row"), CORES)
    out = jnp.dot(group(block_ref, core), own_ref[...], preferred_element_type=F32)
    out += jnp.dot(group(block_ref, 1 - core), other_ref[...], preferred_element_type=F32)
    out_ref[...] = out.astype(out_ref.dtype)


def mixed_term(block, own, other, dtype, cost=SMALL):
    return pl.pallas_call(
        term_kernel,
        out_shape=jax.ShapeDtypeStruct((block.shape[0], own.shape[1]), dtype),
        compiler_params=pltpu.CompilerParams(vmem_limit_bytes=20 * 2**20),
        cost_estimate=cost,
        name="mixed_term",
    )(block, own, other)


def weight_grad_kernel(n, *refs):
    head_refs, grad_refs, total_refs, out_ref = refs[:n], refs[n : 2 * n], refs[2 * n : -1], refs[-1]
    width = out_ref.shape[1] // 4
    for i in range(4):
        columns = pl.ds(i * width, width)
        total = sum(tn(h[...], g[:, columns]) for h, g in zip(head_refs, grad_refs))
        for total_ref in total_refs:
            total = total + total_ref[:, columns].astype(F32)
        out_ref[:, columns] = total.astype(BF16)


def weight_grad_part(heads, grads, *total):
    return pl.pallas_call(
        functools.partial(weight_grad_kernel, len(heads)),
        out_shape=jax.ShapeDtypeStruct((heads[0].shape[1], grads[0].shape[1]), BF16),
        compiler_params=pltpu.CompilerParams(vmem_limit_bytes=28 * 2**20),
        cost_estimate=WINDOW,
        name="weight_grad",
    )(*heads, *grads, *total)


def unpack_kernel(*refs):
    in_refs, out_refs = refs[:COLS], refs[COLS:]
    tokens = out_refs[0].shape[0]
    half = tokens // 2
    col = lax.axis_index("col")
    for j, in_ref in enumerate(in_refs):
        of = lax.bitwise_xor(col, j)
        y, x = lax.div(of, 2), lax.rem(of, 2)
        a = pl.ds(pl.multiple_of((3 * y + x) * HD, HD), HD)
        b = pl.ds(pl.multiple_of((3 * y + 2) * HD, HD), HD)
        out_refs[0][:, a] = in_ref[:tokens]
        out_refs[0][pl.ds(pl.multiple_of(x * half, half), half), b] = in_ref[tokens : tokens + half]
        for i in range(2):
            at = tokens + half + 2 * i * tokens
            out_refs[1 + i][:, a] = in_ref[at : at + tokens]
    for y in range(2):
        b = pl.ds((3 * y + 2) * HD, HD)
        for i in range(2):
            at = tokens + half + (2 * i + 1) * tokens

            def load(x):
                entry = lax.bitwise_xor(col, 2 * y + x)
                block = in_refs[0][at : at + tokens].astype(F32)
                for j in range(1, COLS):
                    block = jnp.where(entry == j, in_refs[j][at : at + tokens].astype(F32), block)
                return block

            out_refs[1 + i][:, b] = (load(0) + load(1)).astype(BF16)


def unpack(blocks, tokens, width):
    return pl.pallas_call(
        unpack_kernel,
        out_shape=[jax.ShapeDtypeStruct((tokens, width), BF16)] * 3,
        cost_estimate=SMALL,
        name="unpack_outputs",
    )(*blocks)


def fence_kernel(in_ref, out_ref):
    del in_ref, out_ref


def fence(*earlier):
    mark = lax.optimization_barrier((jnp.zeros((8, 128), F32), earlier))[0]
    return pl.pallas_call(
        fence_kernel,
        in_specs=[pl.BlockSpec(memory_space=pl.ANY)],
        out_specs=pl.BlockSpec(memory_space=pl.ANY),
        out_shape=jax.ShapeDtypeStruct(mark.shape, mark.dtype),
        compiler_params=pltpu.CompilerParams(has_side_effects=True),
        cost_estimate=WINDOW,
        name="fence",
    )(mark)


def fence0(mark):
    return pl.pallas_call(
        fence_kernel,
        in_specs=[pl.BlockSpec(memory_space=pl.ANY)],
        out_specs=pl.BlockSpec(memory_space=pl.ANY),
        out_shape=jax.ShapeDtypeStruct((8, 128), F32),
        compiler_params=pltpu.CompilerParams(has_side_effects=True),
        cost_estimate=WINDOW,
        name="fence",
    )(mark)


def after(value, *earlier):
    return lax.optimization_barrier((value, earlier))[0]


def per_device_fast(queries, keys_tile, values_tile, out_weight, out_grad):
    tokens = queries.shape[0]
    half = tokens // 2
    own = PLANES * tokens
    width = out_weight.shape[0]
    row, col = lax.axis_index("row"), lax.axis_index("col")
    plane, core = row // CORES, row % CORES

    def head(block, g):
        return block[:, g * HD : (g + 1) * HD]

    def to_col(block, j):
        return lax.ppermute(block, "col", col_xor(j))

    def to_plane(block, s):
        return lax.ppermute(block, "row", row_shift(s))

    def swap(block):
        return lax.ppermute(block, "row", SWAP)

    grad_1 = to_plane(out_grad, 1)
    grad_3 = to_plane(out_grad, -1)
    weights = (out_weight, swap(out_weight))

    pieces = pack(*after((queries, keys_tile, values_tile), fence0(queries)))
    pieces = after(pieces, weights[1])
    moved = after([to_col(pieces[j], j) for j in (1, 2, 3)], fence(pieces))
    over_col = jnp.stack([pieces[0], *moved])

    arrived = [pick(over_col, col ^ plane)]
    for s in ORDER[1:]:
        arrived.append(to_plane(pick(over_col, col ^ ((plane + s) % PLANES)), s))

    early = grad_pieces((out_grad, grad_1, grad_3), *weights)
    early = list(early)
    early[1:] = [to_col(block, j) for j, block in enumerate(after(early[1:], arrived[1]), 1)]

    own_part = after(arrived, early)
    other_part = [swap(block) for block in (*arrived[:3], own_part[3])]
    other_part = after(other_part, fence(own_part))

    grad_2 = to_plane(after(grad_1, arrived), 1)
    grads = [out_grad, grad_1, grad_3, grad_2]

    probs, attn, q, k, v = attention_forward(own_part, other_part, tokens)
    grad_2 = after(grad_2, attn)
    early = [sum(t.astype(F32) for t in after(early, attn)).astype(BF16)]

    def plane_heads(rows, every):
        by_col = [pick(every, col ^ d) for d in range(COLS)]
        columns = []
        for y in range(2):
            columns += [by_col[2 * y][:rows], by_col[2 * y + 1][:rows]]
            halves = [by_col[2 * y + x][rows:].reshape(-1, half, HD) for x in range(2)]
            columns.append(jnp.concatenate(halves, axis=1).reshape(rows, HD))
        return jnp.concatenate(columns, axis=1)

    attn_a, attn_b = attn[:own], attn[own:]
    sent = jnp.concatenate([attn_a[3 * tokens :], attn_b[3 * half :]])
    late = grad_pieces((grad_2,), *weights)
    got = after([to_col(sent, j) for j in (1, 2, 3)], late)
    heads_2 = plane_heads(tokens, jnp.stack([sent, *got]))
    term_2 = mixed_term(heads_2, *weights, BF16)
    mixed_2 = to_plane(term_2, 1)
    late = [late[0]] + [to_col(late[j], j) for j in (1, 2, 3)]
    sent = jnp.concatenate([attn_a[: 3 * tokens], attn_b[: 3 * half]])
    pair = jnp.stack([sent, to_col(sent, 1)])
    rest = [pair, to_col(pair, 2)]

    dq, dkv, dkv_other = attention_backward(q, k, v, probs, attn, early, late)
    rest, mixed_2 = after((rest, mixed_2), dq)

    dkv_other = jnp.stack([jnp.stack([swap(dkv_other[i, h]) for h in range(2)]) for i in range(2)])
    dkv = dkv + dkv_other.astype(F32)
    dkv = dkv.astype(BF16).reshape(4, PLANES, tokens, HD)
    dq_a = dq[:own].reshape(PLANES, tokens, HD)
    dq_b = dq[own:].reshape(PLANES, half, HD)
    home = [
        jnp.concatenate([dq_a[p], dq_b[p]] + [dkv[i, p] for i in range(4)])
        for p in (ORDER.index(s) for s in range(PLANES))
    ]

    away = [to_plane(home[s], -s) for s in range(1, PLANES)]

    heads_rest = plane_heads(3 * tokens, jnp.concatenate(rest))
    heads = [heads_rest[p * tokens : (p + 1) * tokens] for p in range(3)] + [heads_2]
    ours, theirs = [
        [lax.dynamic_slice_in_dim(h, g * width, width, 1) for h in heads] for g in (core, 1 - core)
    ]
    total = weight_grad_part(after(theirs, home), grads)

    head_0, head_1, head_3 = after(heads[:3], total)
    term_1 = mixed_term(head_1, *weights, BF16)
    term_3 = (mixed_2.astype(F32) + mixed_term(head_3, *weights, F32)).astype(BF16)
    total = swap(total)
    term_0 = mixed_term(after(head_0, term_1, term_3), *weights, F32, WINDOW)

    away, total = after((away, total), term_0)
    home = [home[0], *away]
    weight_grad = weight_grad_part(after(ours, home), grads, total)

    mixed_1 = to_plane(after(term_1, home), -1)
    mixed_3 = to_plane(after(term_3, home), 1)

    home = after(jnp.stack(home), weight_grad)
    back = [pick(home, (col - plane) % PLANES)] + [
        to_col(pick(home, ((col ^ j) - plane) % PLANES), j) for j in (1, 2, 3)
    ]
    query_g, key_g, value_g = unpack(back, tokens, queries.shape[1])
    mixed_1, mixed_3 = after((mixed_1, mixed_3), query_g)
    mixed = (term_0 + mixed_1.astype(F32) + mixed_3.astype(F32)).astype(BF16)
    return (mixed, query_g, key_g, value_g, weight_grad)


def solution(mesh):
    spec = P("row", "col")
    fast = mesh.shape["row"] == PLANES * CORES and mesh.shape["col"] == COLS

    def run(queries, keys_tile, values_tile, out_weight, out_grad):
        heads = queries.shape[1] // HD
        fits = fast and heads == 6 * COLS and queries.shape[0] % (32 * mesh.shape["row"]) == 0
        return jax.shard_map(
            per_device_fast if fits else per_device,
            mesh=mesh,
            in_specs=(spec,) * 5,
            out_specs=(spec,) * 5,
            check_vma=False,
        )(queries, keys_tile, values_tile, out_weight, out_grad)

    return run
```

```python
import functools

import jax
import jax.numpy as jnp
from jax import lax
from jax.experimental import pallas as pl
from jax.experimental.pallas import tpu as pltpu
from jax.sharding import PartitionSpec as P

HD = 128
SCALE = HD ** (-0.5)
LOG2E = 1.4426950408889634
F32 = jnp.float32
BF16 = jnp.bfloat16


def head_forward(args):
    query_head, key_head, value_head = args
    scores = jnp.einsum(
        "qd,kd->qk", query_head, key_head, preferred_element_type=jnp.float32
    ) * HD ** (-0.5)
    top = jnp.max(scores, axis=1, keepdims=True)
    lse = top[:, 0] + jnp.log(jnp.sum(jnp.exp(scores - top), axis=1))
    probs = jnp.exp(scores - lse[:, None]).astype(jnp.bfloat16)
    attn = jnp.dot(probs, value_head, preferred_element_type=jnp.float32).astype(jnp.bfloat16)
    return (attn, lse)


def score_grads(query_head, key_head, value_head, grad_head, lse, delta):
    scores = jnp.einsum(
        "qd,kd->qk", query_head, key_head, preferred_element_type=jnp.float32
    ) * HD ** (-0.5)
    probs = jnp.exp(scores - lse[:, None]).astype(jnp.bfloat16)
    dprob = jnp.einsum("qd,kd->qk", grad_head, value_head, preferred_element_type=jnp.float32)
    dscore = (probs.astype(jnp.float32) * (dprob - delta[:, None]) * HD ** (-0.5)).astype(
        jnp.bfloat16
    )
    return (probs, dscore)


def split_heads(block):
    return block.reshape(block.shape[0], block.shape[1] // HD, HD).transpose(1, 0, 2)


def merge_heads(block):
    return block.transpose(1, 0, 2).reshape(block.shape[1], block.shape[0] * HD)


def per_device(queries, keys_tile, values_tile, out_weight, out_grad):
    query3 = split_heads(queries)
    key_local = split_heads(keys_tile)
    value_local = split_heads(values_tile)
    key_every, value_every = (
        lax.all_gather(key_local, "row", axis=1, tiled=True),
        lax.all_gather(value_local, "row", axis=1, tiled=True),
    )
    attn3, lse = lax.map(head_forward, (query3, key_every, value_every))
    attn = merge_heads(attn3)
    attn_row = lax.all_gather(attn, "col", axis=1, tiled=True)
    weight_col = lax.all_gather(out_weight, "row", axis=0, tiled=True)
    mixed = jnp.dot(attn_row, weight_col, preferred_element_type=jnp.float32).astype(jnp.bfloat16)
    partial_grad = jnp.einsum("rc,fc->rf", out_grad, weight_col, preferred_element_type=jnp.float32)
    d_attn = lax.psum_scatter(partial_grad, "col", scatter_dimension=1, tiled=True).astype(
        jnp.bfloat16
    )
    weight_grad = lax.psum_scatter(
        jnp.einsum("rf,rc->fc", attn_row, out_grad, preferred_element_type=jnp.float32).astype(
            jnp.bfloat16
        ),
        "row",
        scatter_dimension=0,
        tiled=True,
    )
    grad3 = split_heads(d_attn)
    delta = jnp.sum(grad3.astype(jnp.float32) * attn3.astype(jnp.float32), axis=2)

    def head_backward(args):
        query_head, key_head, value_head, grad_head, lse_head, delta_head = args
        probs, dscore = score_grads(
            query_head, key_head, value_head, grad_head, lse_head, delta_head
        )
        query_g = jnp.dot(dscore, key_head, preferred_element_type=jnp.float32).astype(jnp.bfloat16)
        key_term = jnp.einsum("qk,qd->kd", dscore, query_head, preferred_element_type=jnp.float32)
        value_term = jnp.einsum("qk,qd->kd", probs, grad_head, preferred_element_type=jnp.float32)
        return (query_g, key_term, value_term)

    query_g3, key_terms, value_terms = lax.map(
        head_backward, (query3, key_every, value_every, grad3, lse, delta)
    )
    key_g3, value_g3 = (
        lax.psum_scatter(key_terms, "row", scatter_dimension=1, tiled=True),
        lax.psum_scatter(value_terms, "row", scatter_dimension=1, tiled=True),
    )
    key_g3 = key_g3.astype(jnp.bfloat16)
    value_g3 = value_g3.astype(jnp.bfloat16)
    return (mixed, merge_heads(query_g3), merge_heads(key_g3), merge_heads(value_g3), weight_grad)


PLANES, CORES, COLS = 4, 2, 4
ORDER = (0, 1, 3, 2)
WINDOW = pl.CostEstimate(flops=4 * 10**10, bytes_accessed=0, transcendentals=0)
SMALL = pl.CostEstimate(flops=10**6, bytes_accessed=10**3, transcendentals=0)


def row_shift(s):
    return [
        (CORES * z + k, CORES * ((z + s) % PLANES) + k)
        for z in range(PLANES)
        for k in range(CORES)
    ]


SWAP = [(CORES * z + k, CORES * z + 1 - k) for z in range(PLANES) for k in range(CORES)]


def col_xor(j):
    return [(c, c ^ j) for c in range(COLS)]


def pick(stack, index):
    return lax.dynamic_index_in_dim(stack, index, 0, keepdims=False)


def nt(a, b):
    return lax.dot_general(a, b, (((1,), (1,)), ((), ())), preferred_element_type=F32)


def tn(a, b):
    return lax.dot_general(a, b, (((0,), (0,)), ((), ())), preferred_element_type=F32)


def forward_kernel(*refs):
    own_refs, other_refs, (p_ref, attn_ref, q_ref, k_ref, v_ref) = refs[:PLANES], refs[PLANES:-5], refs[-5:]
    step = pl.program_id(0)
    rows = attn_ref.shape[0]

    @pl.when(step == 0)
    def _():
        tokens = k_ref.shape[1] // (2 * PLANES)
        half = tokens // 2
        for p, own_ref in enumerate(own_refs):
            q_ref[p * tokens : (p + 1) * tokens] = own_ref[:tokens]
            at = PLANES * tokens + p * half
            q_ref[at : at + half] = own_ref[tokens : tokens + half]
        for p, in_ref in enumerate(own_refs + other_refs):
            for i in range(4):
                at = tokens + half + i * tokens
                out_ref = (k_ref, v_ref)[i // 2]
                out_ref[i % 2, p * tokens : (p + 1) * tokens] = in_ref[at : at + tokens]

    head = lax.div(step, 2)
    raw = nt(k_ref[head], q_ref[pl.ds(pl.multiple_of(step * rows, rows), rows)])
    top = jnp.max(raw, axis=0, keepdims=True)
    e = jnp.exp2((raw - top) * (SCALE * LOG2E))
    total = jnp.sum(e, axis=0, keepdims=True)
    probs = (e * (1.0 / total)).astype(BF16)
    p_ref[0] = probs
    attn_ref[...] = tn(v_ref[head], probs).T.astype(BF16)


def attention_forward(own, other, tokens):
    rows, keys = 2 * tokens, 2 * PLANES * tokens

    def whole(*shape):
        return pl.BlockSpec(shape, lambda i: (0,) * len(shape))

    return pl.pallas_call(
        forward_kernel,
        grid=(3,),
        in_specs=[whole(*own[0].shape)] * (2 * PLANES),
        out_specs=[
            pl.BlockSpec((1, keys, rows), lambda i: (i, 0, 0)),
            pl.BlockSpec((rows, HD), lambda i: (i, 0)),
            whole(3 * rows, HD),
            whole(2, keys, HD),
            whole(2, keys, HD),
        ],
        out_shape=[
            pltpu.HBM((3, keys, rows), BF16),
            jax.ShapeDtypeStruct((3 * rows, HD), BF16),
            jax.ShapeDtypeStruct((3 * rows, HD), BF16),
            jax.ShapeDtypeStruct((2, keys, HD), BF16),
            jax.ShapeDtypeStruct((2, keys, HD), BF16),
        ],
        compiler_params=pltpu.CompilerParams(vmem_limit_bytes=24 * 2**20),
        cost_estimate=WINDOW,
        name="attention_forward",
    )(*own, *other)


def backward_kernel(
    q_ref, k_ref, v_ref, p_ref, attn_ref, *refs
):
    early_refs, late_refs, refs = refs[:1], refs[1 : 1 + COLS], refs[1 + COLS :]
    dq_ref, own_ref, other_ref, grad_ref, sums_ref = refs
    step = pl.program_id(0)
    rows = q_ref.shape[0]

    @pl.when(step == 0)
    def _():
        early_a, late_a = early_refs[0].shape[0] * 2 // 3, late_refs[0].shape[0] * 2 // 3
        early = early_refs[0][...]
        late = sum(ref[...].astype(F32) for ref in late_refs).astype(BF16)
        own = early_a + late_a
        grad_ref[:early_a] = early[:early_a]
        grad_ref[early_a:own] = late[:late_a]
        grad_ref[own : own + early_a // 2] = early[early_a:]
        grad_ref[own + early_a // 2 :] = late[late_a:]

    grad = grad_ref[pl.ds(pl.multiple_of(step * rows, rows), rows)]
    product = grad.astype(F32) * attn_ref[...].astype(F32)
    delta = jnp.sum(product.T, axis=0, keepdims=True)
    probs = p_ref[0]
    dprob = nt(v_ref[0], grad)
    dscore = (probs.astype(F32) * (dprob - delta) * SCALE).astype(BF16)
    dq_ref[...] = tn(k_ref[0], dscore).T.astype(BF16)
    dk = jnp.dot(dscore, q_ref[...], preferred_element_type=F32)
    dv = jnp.dot(probs, grad, preferred_element_type=F32)

    @pl.when(step == 0)
    def _():
        sums_ref[0] = dk
        sums_ref[1] = dv

    @pl.when(step != 0)
    def _():
        half = dk.shape[0] // 2
        for i, new in enumerate((dk, dv)):
            new = jnp.where(step == 1, sums_ref[i], 0.0) + new
            own_ref[i, 0] = new[:half]
            other_ref[i, 0] = new[half:].astype(BF16)


def attention_backward(q, k, v, probs, attn, early, late):
    rows, keys = q.shape[0] // 3, k.shape[1]
    by_query = pl.BlockSpec((rows, HD), lambda i: (i, 0))
    by_head = pl.BlockSpec((1, keys, HD), lambda i: (i // 2, 0, 0))
    by_half = pl.BlockSpec((2, 1, keys // 2, HD), lambda i: (0, i // 2, 0, 0))
    return pl.pallas_call(
        backward_kernel,
        grid=(3,),
        in_specs=[
            by_query,
            by_head,
            by_head,
            pl.BlockSpec((1, keys, rows), lambda i: (i, 0, 0)),
            by_query,
            *[pl.BlockSpec(block.shape, lambda i: (0, 0)) for block in (*early, *late)],
        ],
        out_specs=[by_query, by_half, by_half],
        out_shape=[
            jax.ShapeDtypeStruct(q.shape, BF16),
            jax.ShapeDtypeStruct((2, 2, keys // 2, HD), F32),
            jax.ShapeDtypeStruct((2, 2, keys // 2, HD), BF16),
        ],
        scratch_shapes=[pltpu.VMEM(q.shape, BF16), pltpu.VMEM((2, keys, HD), F32)],
        compiler_params=pltpu.CompilerParams(vmem_limit_bytes=20 * 2**20),
        cost_estimate=WINDOW,
        name="attention_backward",
    )(q, k, v, probs, attn, *early, *late)


def pack_kernel(q_ref, k_ref, v_ref, *out_refs):
    tokens = q_ref.shape[0]
    half = tokens // 2
    col = lax.axis_index("col")
    for j, out_ref in enumerate(out_refs):
        to = lax.bitwise_xor(col, j)
        y, x = lax.div(to, 2), lax.rem(to, 2)
        a = pl.ds(pl.multiple_of((3 * y + x) * HD, HD), HD)
        b = pl.ds(pl.multiple_of((3 * y + 2) * HD, HD), HD)
        at = tokens + half
        out_ref[:tokens] = q_ref[:, a]
        out_ref[tokens:at] = q_ref[pl.ds(pl.multiple_of(x * half, half), half), b]
        for i, block in enumerate((k_ref[:, a], k_ref[:, b], v_ref[:, a], v_ref[:, b])):
            out_ref[at + i * tokens : at + (i + 1) * tokens] = block


def pack(queries, keys, values):
    tokens = queries.shape[0]
    piece = jax.ShapeDtypeStruct((tokens // 2 + 5 * tokens, HD), BF16)
    return pl.pallas_call(
        pack_kernel,
        out_shape=[piece] * COLS,
        cost_estimate=WINDOW,
        name="pack_inputs",
    )(queries, keys, values)


def grad_kernel(*refs):
    n = len(refs) - 2 - COLS - 1
    own_ref, other_ref = refs[n : n + 2]
    out_refs, part_ref = refs[n + 2 : -1], refs[-1]
    tokens = refs[0].shape[0]
    half = tokens // 2
    core, col = lax.rem(lax.axis_index("row"), CORES), lax.axis_index("col")
    for i in range(n):
        rows = pl.ds(i * tokens, tokens)
        block = refs[i][...]
        part_ref[core, rows] = nt(block, own_ref[...]).astype(BF16)
        part_ref[1 - core, rows] = nt(block, other_ref[...]).astype(BF16)
    for j, out_ref in enumerate(out_refs):
        to = lax.bitwise_xor(col, j)
        y, x = lax.div(to, 2), lax.rem(to, 2)
        out_ref[: n * tokens] = part_ref[y, :, pl.ds(pl.multiple_of(x * HD, HD), HD)]
        for i in range(n):
            rows = pl.ds(pl.multiple_of(i * tokens + x * half, half), half)
            out_ref[pl.ds(n * tokens + i * half, half)] = part_ref[y, rows, 2 * HD : 3 * HD]


def grad_pieces(blocks, own, other, cost=WINDOW):
    rows = len(blocks) * blocks[0].shape[0]
    piece = jax.ShapeDtypeStruct((rows + rows // 2, HD), BF16)
    return pl.pallas_call(
        grad_kernel,
        out_shape=[piece] * COLS,
        scratch_shapes=[pltpu.VMEM((CORES, rows, own.shape[0]), BF16)],
        compiler_params=pltpu.CompilerParams(vmem_limit_bytes=20 * 2**20),
        cost_estimate=cost,
        name="grad_pieces",
    )(*blocks, own, other)


def group(ref, index):
    width = ref.shape[1] // CORES
    return ref[:, pl.ds(pl.multiple_of(index * width, width), width)]


def term_kernel(block_ref, own_ref, other_ref, out_ref):
    core = lax.rem(lax.axis_index("row"), CORES)
    out = jnp.dot(group(block_ref, core), own_ref[...], preferred_element_type=F32)
    out += jnp.dot(group(block_ref, 1 - core), other_ref[...], preferred_element_type=F32)
    out_ref[...] = out.astype(out_ref.dtype)


def mixed_term(block, own, other, dtype, cost=SMALL):
    return pl.pallas_call(
        term_kernel,
        out_shape=jax.ShapeDtypeStruct((block.shape[0], own.shape[1]), dtype),
        compiler_params=pltpu.CompilerParams(vmem_limit_bytes=20 * 2**20),
        cost_estimate=cost,
        name="mixed_term",
    )(block, own, other)


def weight_grad_kernel(n, *refs):
    head_refs, grad_refs, total_refs, out_ref = refs[:n], refs[n : 2 * n], refs[2 * n : -1], refs[-1]
    width = out_ref.shape[1] // 4
    for i in range(4):
        columns = pl.ds(i * width, width)
        total = sum(tn(h[...], g[:, columns]) for h, g in zip(head_refs, grad_refs))
        for total_ref in total_refs:
            total = total + total_ref[:, columns].astype(F32)
        out_ref[:, columns] = total.astype(BF16)


def weight_grad_part(heads, grads, *total):
    return pl.pallas_call(
        functools.partial(weight_grad_kernel, len(heads)),
        out_shape=jax.ShapeDtypeStruct((heads[0].shape[1], grads[0].shape[1]), BF16),
        compiler_params=pltpu.CompilerParams(vmem_limit_bytes=28 * 2**20),
        cost_estimate=WINDOW,
        name="weight_grad",
    )(*heads, *grads, *total)


def unpack_kernel(*refs):
    in_refs, out_refs = refs[:COLS], refs[COLS:]
    tokens = out_refs[0].shape[0]
    half = tokens // 2
    col = lax.axis_index("col")
    for j, in_ref in enumerate(in_refs):
        of = lax.bitwise_xor(col, j)
        y, x = lax.div(of, 2), lax.rem(of, 2)
        a = pl.ds(pl.multiple_of((3 * y + x) * HD, HD), HD)
        b = pl.ds(pl.multiple_of((3 * y + 2) * HD, HD), HD)
        out_refs[0][:, a] = in_ref[:tokens]
        out_refs[0][pl.ds(pl.multiple_of(x * half, half), half), b] = in_ref[tokens : tokens + half]
        for i in range(2):
            at = tokens + half + 2 * i * tokens
            out_refs[1 + i][:, a] = in_ref[at : at + tokens]
    for y in range(2):
        b = pl.ds((3 * y + 2) * HD, HD)
        for i in range(2):
            at = tokens + half + (2 * i + 1) * tokens

            def load(x):
                entry = lax.bitwise_xor(col, 2 * y + x)
                block = in_refs[0][at : at + tokens].astype(F32)
                for j in range(1, COLS):
                    block = jnp.where(entry == j, in_refs[j][at : at + tokens].astype(F32), block)
                return block

            out_refs[1 + i][:, b] = (load(0) + load(1)).astype(BF16)


def unpack(blocks, tokens, width):
    return pl.pallas_call(
        unpack_kernel,
        out_shape=[jax.ShapeDtypeStruct((tokens, width), BF16)] * 3,
        cost_estimate=SMALL,
        name="unpack_outputs",
    )(*blocks)


def fence_kernel(in_ref, out_ref):
    del in_ref, out_ref


def fence(*earlier):
    mark = lax.optimization_barrier((jnp.zeros((8, 128), F32), earlier))[0]
    return pl.pallas_call(
        fence_kernel,
        in_specs=[pl.BlockSpec(memory_space=pl.ANY)],
        out_specs=pl.BlockSpec(memory_space=pl.ANY),
        out_shape=jax.ShapeDtypeStruct(mark.shape, mark.dtype),
        compiler_params=pltpu.CompilerParams(has_side_effects=True),
        cost_estimate=WINDOW,
        name="fence",
    )(mark)


def fence0(mark):
    return pl.pallas_call(
        fence_kernel,
        in_specs=[pl.BlockSpec(memory_space=pl.ANY)],
        out_specs=pl.BlockSpec(memory_space=pl.ANY),
        out_shape=jax.ShapeDtypeStruct((8, 128), F32),
        compiler_params=pltpu.CompilerParams(has_side_effects=True),
        cost_estimate=WINDOW,
        name="fence",
    )(mark)


def after(value, *earlier):
    return lax.optimization_barrier((value, earlier))[0]


def per_device_fast(queries, keys_tile, values_tile, out_weight, out_grad):
    tokens = queries.shape[0]
    half = tokens // 2
    own = PLANES * tokens
    width = out_weight.shape[0]
    row, col = lax.axis_index("row"), lax.axis_index("col")
    plane, core = row // CORES, row % CORES

    def head(block, g):
        return block[:, g * HD : (g + 1) * HD]

    def to_col(block, j):
        return lax.ppermute(block, "col", col_xor(j))

    def to_plane(block, s):
        return lax.ppermute(block, "row", row_shift(s))

    def swap(block):
        return lax.ppermute(block, "row", SWAP)

    grad_1 = to_plane(out_grad, 1)
    grad_3 = to_plane(out_grad, -1)
    weights = (out_weight, swap(out_weight))

    pieces = pack(*after((queries, keys_tile, values_tile), fence0(queries)))
    pieces = after(pieces, weights[1])
    moved = after([to_col(pieces[j], j) for j in (1, 2, 3)], fence(pieces))
    over_col = jnp.stack([pieces[0], *moved])

    arrived = [pick(over_col, col ^ plane)]
    for s in ORDER[1:]:
        arrived.append(to_plane(pick(over_col, col ^ ((plane + s) % PLANES)), s))

    early = grad_pieces((out_grad, grad_1, grad_3), *weights)
    early = list(early)
    early[1:] = [to_col(block, j) for j, block in enumerate(after(early[1:], arrived[1]), 1)]

    own_part = after(arrived, early)
    other_part = [swap(block) for block in (*arrived[:3], own_part[3])]
    other_part = after(other_part, fence(own_part))

    grad_2 = to_plane(after(grad_1, arrived), 1)
    grads = [out_grad, grad_1, grad_3, grad_2]

    probs, attn, q, k, v = attention_forward(own_part, other_part, tokens)
    grad_2 = after(grad_2, attn)
    early = [sum(t.astype(F32) for t in after(early, attn)).astype(BF16)]

    def plane_heads(rows, every):
        by_col = [pick(every, col ^ d) for d in range(COLS)]
        columns = []
        for y in range(2):
            columns += [by_col[2 * y][:rows], by_col[2 * y + 1][:rows]]
            halves = [by_col[2 * y + x][rows:].reshape(-1, half, HD) for x in range(2)]
            columns.append(jnp.concatenate(halves, axis=1).reshape(rows, HD))
        return jnp.concatenate(columns, axis=1)

    attn_a, attn_b = attn[:own], attn[own:]
    sent = jnp.concatenate([attn_a[3 * tokens :], attn_b[3 * half :]])
    late = grad_pieces((grad_2,), *weights)
    got = after([to_col(sent, j) for j in (1, 2, 3)], late)
    heads_2 = plane_heads(tokens, jnp.stack([sent, *got]))
    term_2 = mixed_term(heads_2, *weights, BF16)
    mixed_2 = to_plane(term_2, 1)
    late = [late[0]] + [to_col(late[j], j) for j in (1, 2, 3)]
    sent = jnp.concatenate([attn_a[: 3 * tokens], attn_b[: 3 * half]])
    pair = jnp.stack([sent, to_col(sent, 1)])
    rest = [pair, to_col(pair, 2)]

    dq, dkv, dkv_other = attention_backward(q, k, v, probs, attn, early, late)
    rest, mixed_2 = after((rest, mixed_2), dq)

    dkv_other = jnp.stack([jnp.stack([swap(dkv_other[i, h]) for h in range(2)]) for i in range(2)])
    dkv = dkv + dkv_other.astype(F32)
    dkv = dkv.astype(BF16).reshape(4, PLANES, tokens, HD)
    dq_a = dq[:own].reshape(PLANES, tokens, HD)
    dq_b = dq[own:].reshape(PLANES, half, HD)
    home = [
        jnp.concatenate([dq_a[p], dq_b[p]] + [dkv[i, p] for i in range(4)])
        for p in (ORDER.index(s) for s in range(PLANES))
    ]

    away = [to_plane(home[s], -s) for s in range(1, PLANES)]

    heads_rest = plane_heads(3 * tokens, jnp.concatenate(rest))
    heads = [heads_rest[p * tokens : (p + 1) * tokens] for p in range(3)] + [heads_2]
    ours, theirs = [
        [lax.dynamic_slice_in_dim(h, g * width, width, 1) for h in heads] for g in (core, 1 - core)
    ]
    total = weight_grad_part(after(theirs, home), grads)

    head_0, head_1, head_3 = after(heads[:3], total)
    term_1 = mixed_term(head_1, *weights, BF16, WINDOW)
    term_3 = (mixed_2.astype(F32) + mixed_term(head_3, *weights, F32)).astype(BF16)
    total = swap(total)

    weight_grad = weight_grad_part(ours, grads, after(total, term_1, term_3))
    home = [home[0], *after(away, weight_grad)]
    term_0 = mixed_term(after(head_0, home), *weights, F32, WINDOW)

    mixed_1 = to_plane(after(term_1, home), -1)
    mixed_3 = to_plane(after(term_3, home), 1)

    home = after(jnp.stack(home), term_0)
    back = [pick(home, (col - plane) % PLANES)] + [
        to_col(pick(home, ((col ^ j) - plane) % PLANES), j) for j in (1, 2, 3)
    ]
    query_g, key_g, value_g = unpack(back, tokens, queries.shape[1])
    mixed_1, mixed_3 = after((mixed_1, mixed_3), query_g)
    mixed = (term_0 + mixed_1.astype(F32) + mixed_3.astype(F32)).astype(BF16)
    return (mixed, query_g, key_g, value_g, weight_grad)


def solution(mesh):
    spec = P("row", "col")
    fast = mesh.shape["row"] == PLANES * CORES and mesh.shape["col"] == COLS

    def run(queries, keys_tile, values_tile, out_weight, out_grad):
        heads = queries.shape[1] // HD
        fits = fast and heads == 6 * COLS and queries.shape[0] % (32 * mesh.shape["row"]) == 0
        return jax.shard_map(
            per_device_fast if fits else per_device,
            mesh=mesh,
            in_specs=(spec,) * 5,
            out_specs=(spec,) * 5,
            check_vma=False,
        )(queries, keys_tile, values_tile, out_weight, out_grad)

    return run
```

```python
import functools

import jax
import jax.numpy as jnp
from jax import lax
from jax.experimental import pallas as pl
from jax.experimental.pallas import tpu as pltpu
from jax.sharding import PartitionSpec as P

HD = 128
SCALE = HD ** (-0.5)
LOG2E = 1.4426950408889634
F32 = jnp.float32
BF16 = jnp.bfloat16


def head_forward(args):
    query_head, key_head, value_head = args
    scores = jnp.einsum(
        "qd,kd->qk", query_head, key_head, preferred_element_type=jnp.float32
    ) * HD ** (-0.5)
    top = jnp.max(scores, axis=1, keepdims=True)
    lse = top[:, 0] + jnp.log(jnp.sum(jnp.exp(scores - top), axis=1))
    probs = jnp.exp(scores - lse[:, None]).astype(jnp.bfloat16)
    attn = jnp.dot(probs, value_head, preferred_element_type=jnp.float32).astype(jnp.bfloat16)
    return (attn, lse)


def score_grads(query_head, key_head, value_head, grad_head, lse, delta):
    scores = jnp.einsum(
        "qd,kd->qk", query_head, key_head, preferred_element_type=jnp.float32
    ) * HD ** (-0.5)
    probs = jnp.exp(scores - lse[:, None]).astype(jnp.bfloat16)
    dprob = jnp.einsum("qd,kd->qk", grad_head, value_head, preferred_element_type=jnp.float32)
    dscore = (probs.astype(jnp.float32) * (dprob - delta[:, None]) * HD ** (-0.5)).astype(
        jnp.bfloat16
    )
    return (probs, dscore)


def split_heads(block):
    return block.reshape(block.shape[0], block.shape[1] // HD, HD).transpose(1, 0, 2)


def merge_heads(block):
    return block.transpose(1, 0, 2).reshape(block.shape[1], block.shape[0] * HD)


def per_device(queries, keys_tile, values_tile, out_weight, out_grad):
    query3 = split_heads(queries)
    key_local = split_heads(keys_tile)
    value_local = split_heads(values_tile)
    key_every, value_every = (
        lax.all_gather(key_local, "row", axis=1, tiled=True),
        lax.all_gather(value_local, "row", axis=1, tiled=True),
    )
    attn3, lse = lax.map(head_forward, (query3, key_every, value_every))
    attn = merge_heads(attn3)
    attn_row = lax.all_gather(attn, "col", axis=1, tiled=True)
    weight_col = lax.all_gather(out_weight, "row", axis=0, tiled=True)
    mixed = jnp.dot(attn_row, weight_col, preferred_element_type=jnp.float32).astype(jnp.bfloat16)
    partial_grad = jnp.einsum("rc,fc->rf", out_grad, weight_col, preferred_element_type=jnp.float32)
    d_attn = lax.psum_scatter(partial_grad, "col", scatter_dimension=1, tiled=True).astype(
        jnp.bfloat16
    )
    weight_grad = lax.psum_scatter(
        jnp.einsum("rf,rc->fc", attn_row, out_grad, preferred_element_type=jnp.float32).astype(
            jnp.bfloat16
        ),
        "row",
        scatter_dimension=0,
        tiled=True,
    )
    grad3 = split_heads(d_attn)
    delta = jnp.sum(grad3.astype(jnp.float32) * attn3.astype(jnp.float32), axis=2)

    def head_backward(args):
        query_head, key_head, value_head, grad_head, lse_head, delta_head = args
        probs, dscore = score_grads(
            query_head, key_head, value_head, grad_head, lse_head, delta_head
        )
        query_g = jnp.dot(dscore, key_head, preferred_element_type=jnp.float32).astype(jnp.bfloat16)
        key_term = jnp.einsum("qk,qd->kd", dscore, query_head, preferred_element_type=jnp.float32)
        value_term = jnp.einsum("qk,qd->kd", probs, grad_head, preferred_element_type=jnp.float32)
        return (query_g, key_term, value_term)

    query_g3, key_terms, value_terms = lax.map(
        head_backward, (query3, key_every, value_every, grad3, lse, delta)
    )
    key_g3, value_g3 = (
        lax.psum_scatter(key_terms, "row", scatter_dimension=1, tiled=True),
        lax.psum_scatter(value_terms, "row", scatter_dimension=1, tiled=True),
    )
    key_g3 = key_g3.astype(jnp.bfloat16)
    value_g3 = value_g3.astype(jnp.bfloat16)
    return (mixed, merge_heads(query_g3), merge_heads(key_g3), merge_heads(value_g3), weight_grad)


PLANES, CORES, COLS = 4, 2, 4
ORDER = (0, 1, 3, 2)
WINDOW = pl.CostEstimate(flops=4 * 10**10, bytes_accessed=0, transcendentals=0)
SMALL = pl.CostEstimate(flops=10**6, bytes_accessed=10**3, transcendentals=0)


def row_shift(s):
    return [
        (CORES * z + k, CORES * ((z + s) % PLANES) + k)
        for z in range(PLANES)
        for k in range(CORES)
    ]


SWAP = [(CORES * z + k, CORES * z + 1 - k) for z in range(PLANES) for k in range(CORES)]


def col_xor(j):
    return [(c, c ^ j) for c in range(COLS)]


def pick(stack, index):
    return lax.dynamic_index_in_dim(stack, index, 0, keepdims=False)


def nt(a, b):
    return lax.dot_general(a, b, (((1,), (1,)), ((), ())), preferred_element_type=F32)


def tn(a, b):
    return lax.dot_general(a, b, (((0,), (0,)), ((), ())), preferred_element_type=F32)


def forward_kernel(*refs):
    own_refs, other_refs, refs = refs[:PLANES], refs[PLANES : 2 * PLANES], refs[2 * PLANES :]
    p_ref, attn_ref, q_ref, k_ref, v_ref, sems = refs
    step = pl.program_id(0)
    rows = attn_ref.shape[0]

    @pl.when(step == 0)
    def _():
        tokens = k_ref.shape[1] // (2 * PLANES)
        half = tokens // 2
        moves = []
        for p, own_ref in enumerate(own_refs):
            moves.append((own_ref, 0, tokens, q_ref, p * tokens))
            moves.append((own_ref, tokens, half, q_ref, PLANES * tokens + p * half))
        for p, in_ref in enumerate(own_refs + other_refs):
            for i in range(4):
                out_ref = (k_ref, v_ref)[i // 2].at[i % 2]
                moves.append((in_ref, tokens + half + i * tokens, tokens, out_ref, p * tokens))
        copies = [
            pltpu.make_async_copy(
                in_ref.at[pl.ds(at, n)], out_ref.at[pl.ds(to, n)], sems.at[i]
            )
            for i, (in_ref, at, n, out_ref, to) in enumerate(moves)
        ]
        for copy in copies:
            copy.start()
        for copy in copies:
            copy.wait()

    head = lax.div(step, 2)
    raw = nt(k_ref[head], q_ref[pl.ds(pl.multiple_of(step * rows, rows), rows)])
    top = jnp.max(raw, axis=0, keepdims=True)
    e = jnp.exp2((raw - top) * (SCALE * LOG2E))
    total = jnp.sum(e, axis=0, keepdims=True)
    probs = (e * (1.0 / total)).astype(BF16)
    p_ref[0] = probs
    attn_ref[...] = tn(v_ref[head], probs).T.astype(BF16)


def attention_forward(own, other, tokens):
    rows, keys = 2 * tokens, 2 * PLANES * tokens

    def whole(*shape):
        return pl.BlockSpec(shape, lambda i: (0,) * len(shape))

    return pl.pallas_call(
        forward_kernel,
        grid=(3,),
        in_specs=[pl.BlockSpec(memory_space=pl.ANY)] * (2 * PLANES),
        scratch_shapes=[pltpu.SemaphoreType.DMA((10 * PLANES,))],
        out_specs=[
            pl.BlockSpec((1, keys, rows), lambda i: (i, 0, 0)),
            pl.BlockSpec((rows, HD), lambda i: (i, 0)),
            whole(3 * rows, HD),
            whole(2, keys, HD),
            whole(2, keys, HD),
        ],
        out_shape=[
            pltpu.HBM((3, keys, rows), BF16),
            jax.ShapeDtypeStruct((3 * rows, HD), BF16),
            jax.ShapeDtypeStruct((3 * rows, HD), BF16),
            jax.ShapeDtypeStruct((2, keys, HD), BF16),
            jax.ShapeDtypeStruct((2, keys, HD), BF16),
        ],
        compiler_params=pltpu.CompilerParams(vmem_limit_bytes=24 * 2**20),
        cost_estimate=WINDOW,
        name="attention_forward",
    )(*own, *other)


def backward_kernel(
    q_ref, k_ref, v_ref, p_ref, attn_ref, *refs
):
    early_refs, late_refs, refs = refs[:1], refs[1 : 1 + COLS], refs[1 + COLS :]
    dq_ref, own_ref, other_ref, grad_ref, sums_ref = refs
    step = pl.program_id(0)
    rows = q_ref.shape[0]

    @pl.when(step == 0)
    def _():
        early_a, late_a = early_refs[0].shape[0] * 2 // 3, late_refs[0].shape[0] * 2 // 3
        early = early_refs[0][...]
        late = sum(ref[...].astype(F32) for ref in late_refs).astype(BF16)
        own = early_a + late_a
        grad_ref[:early_a] = early[:early_a]
        grad_ref[early_a:own] = late[:late_a]
        grad_ref[own : own + early_a // 2] = early[early_a:]
        grad_ref[own + early_a // 2 :] = late[late_a:]

    grad = grad_ref[pl.ds(pl.multiple_of(step * rows, rows), rows)]
    product = grad.astype(F32) * attn_ref[...].astype(F32)
    delta = jnp.sum(product.T, axis=0, keepdims=True)
    probs = p_ref[0]
    dprob = nt(v_ref[0], grad)
    dscore = (probs.astype(F32) * (dprob - delta) * SCALE).astype(BF16)
    dq_ref[...] = tn(k_ref[0], dscore).T.astype(BF16)
    dk = jnp.dot(dscore, q_ref[...], preferred_element_type=F32)
    dv = jnp.dot(probs, grad, preferred_element_type=F32)

    @pl.when(step == 0)
    def _():
        sums_ref[0] = dk
        sums_ref[1] = dv

    @pl.when(step != 0)
    def _():
        half = dk.shape[0] // 2
        for i, new in enumerate((dk, dv)):
            new = jnp.where(step == 1, sums_ref[i], 0.0) + new
            own_ref[i, 0] = new[:half]
            other_ref[i, 0] = new[half:].astype(BF16)


def attention_backward(q, k, v, probs, attn, early, late):
    rows, keys = q.shape[0] // 3, k.shape[1]
    by_query = pl.BlockSpec((rows, HD), lambda i: (i, 0))
    by_head = pl.BlockSpec((1, keys, HD), lambda i: (i // 2, 0, 0))
    by_half = pl.BlockSpec((2, 1, keys // 2, HD), lambda i: (0, i // 2, 0, 0))
    return pl.pallas_call(
        backward_kernel,
        grid=(3,),
        in_specs=[
            by_query,
            by_head,
            by_head,
            pl.BlockSpec((1, keys, rows), lambda i: (i, 0, 0)),
            by_query,
            *[pl.BlockSpec(block.shape, lambda i: (0, 0)) for block in (*early, *late)],
        ],
        out_specs=[by_query, by_half, by_half],
        out_shape=[
            jax.ShapeDtypeStruct(q.shape, BF16),
            jax.ShapeDtypeStruct((2, 2, keys // 2, HD), F32),
            jax.ShapeDtypeStruct((2, 2, keys // 2, HD), BF16),
        ],
        scratch_shapes=[pltpu.VMEM(q.shape, BF16), pltpu.VMEM((2, keys, HD), F32)],
        compiler_params=pltpu.CompilerParams(vmem_limit_bytes=20 * 2**20),
        cost_estimate=WINDOW,
        name="attention_backward",
    )(q, k, v, probs, attn, *early, *late)


def pack_kernel(q_ref, k_ref, v_ref, *out_refs):
    tokens = q_ref.shape[0]
    half = tokens // 2
    col = lax.axis_index("col")
    for j, out_ref in enumerate(out_refs):
        to = lax.bitwise_xor(col, j)
        y, x = lax.div(to, 2), lax.rem(to, 2)
        a = pl.ds(pl.multiple_of((3 * y + x) * HD, HD), HD)
        b = pl.ds(pl.multiple_of((3 * y + 2) * HD, HD), HD)
        at = tokens + half
        out_ref[:tokens] = q_ref[:, a]
        out_ref[tokens:at] = q_ref[pl.ds(pl.multiple_of(x * half, half), half), b]
        for i, block in enumerate((k_ref[:, a], k_ref[:, b], v_ref[:, a], v_ref[:, b])):
            out_ref[at + i * tokens : at + (i + 1) * tokens] = block


def pack(queries, keys, values):
    tokens = queries.shape[0]
    piece = jax.ShapeDtypeStruct((tokens // 2 + 5 * tokens, HD), BF16)
    return pl.pallas_call(
        pack_kernel,
        out_shape=[piece] * COLS,
        cost_estimate=WINDOW,
        name="pack_inputs",
    )(queries, keys, values)


def grad_kernel(*refs):
    n = len(refs) - 2 - COLS - 1
    own_ref, other_ref = refs[n : n + 2]
    out_refs, part_ref = refs[n + 2 : -1], refs[-1]
    tokens = refs[0].shape[0]
    half = tokens // 2
    core, col = lax.rem(lax.axis_index("row"), CORES), lax.axis_index("col")
    for i in range(n):
        rows = pl.ds(i * tokens, tokens)
        block = refs[i][...]
        part_ref[core, rows] = nt(block, own_ref[...]).astype(BF16)
        part_ref[1 - core, rows] = nt(block, other_ref[...]).astype(BF16)
    for j, out_ref in enumerate(out_refs):
        to = lax.bitwise_xor(col, j)
        y, x = lax.div(to, 2), lax.rem(to, 2)
        out_ref[: n * tokens] = part_ref[y, :, pl.ds(pl.multiple_of(x * HD, HD), HD)]
        for i in range(n):
            rows = pl.ds(pl.multiple_of(i * tokens + x * half, half), half)
            out_ref[pl.ds(n * tokens + i * half, half)] = part_ref[y, rows, 2 * HD : 3 * HD]


def grad_pieces(blocks, own, other, cost=WINDOW):
    rows = len(blocks) * blocks[0].shape[0]
    piece = jax.ShapeDtypeStruct((rows + rows // 2, HD), BF16)
    return pl.pallas_call(
        grad_kernel,
        out_shape=[piece] * COLS,
        scratch_shapes=[pltpu.VMEM((CORES, rows, own.shape[0]), BF16)],
        compiler_params=pltpu.CompilerParams(vmem_limit_bytes=20 * 2**20),
        cost_estimate=cost,
        name="grad_pieces",
    )(*blocks, own, other)


def group(ref, index):
    width = ref.shape[1] // CORES
    return ref[:, pl.ds(pl.multiple_of(index * width, width), width)]


def term_kernel(block_ref, own_ref, other_ref, out_ref):
    core = lax.rem(lax.axis_index("row"), CORES)
    out = jnp.dot(group(block_ref, core), own_ref[...], preferred_element_type=F32)
    out += jnp.dot(group(block_ref, 1 - core), other_ref[...], preferred_element_type=F32)
    out_ref[...] = out.astype(out_ref.dtype)


def mixed_term(block, own, other, dtype, cost=SMALL):
    return pl.pallas_call(
        term_kernel,
        out_shape=jax.ShapeDtypeStruct((block.shape[0], own.shape[1]), dtype),
        compiler_params=pltpu.CompilerParams(vmem_limit_bytes=20 * 2**20),
        cost_estimate=cost,
        name="mixed_term",
    )(block, own, other)


def weight_grad_kernel(n, *refs):
    head_refs, grad_refs, total_refs, out_ref = refs[:n], refs[n : 2 * n], refs[2 * n : -1], refs[-1]
    width = out_ref.shape[1] // 4
    for i in range(4):
        columns = pl.ds(i * width, width)
        total = sum(tn(h[...], g[:, columns]) for h, g in zip(head_refs, grad_refs))
        for total_ref in total_refs:
            total = total + total_ref[:, columns].astype(F32)
        out_ref[:, columns] = total.astype(BF16)


def weight_grad_part(heads, grads, *total):
    return pl.pallas_call(
        functools.partial(weight_grad_kernel, len(heads)),
        out_shape=jax.ShapeDtypeStruct((heads[0].shape[1], grads[0].shape[1]), BF16),
        compiler_params=pltpu.CompilerParams(vmem_limit_bytes=28 * 2**20),
        cost_estimate=WINDOW,
        name="weight_grad",
    )(*heads, *grads, *total)


def unpack_kernel(*refs):
    in_refs, out_refs = refs[:COLS], refs[COLS:]
    tokens = out_refs[0].shape[0]
    half = tokens // 2
    col = lax.axis_index("col")
    for j, in_ref in enumerate(in_refs):
        of = lax.bitwise_xor(col, j)
        y, x = lax.div(of, 2), lax.rem(of, 2)
        a = pl.ds(pl.multiple_of((3 * y + x) * HD, HD), HD)
        b = pl.ds(pl.multiple_of((3 * y + 2) * HD, HD), HD)
        out_refs[0][:, a] = in_ref[:tokens]
        out_refs[0][pl.ds(pl.multiple_of(x * half, half), half), b] = in_ref[tokens : tokens + half]
        for i in range(2):
            at = tokens + half + 2 * i * tokens
            out_refs[1 + i][:, a] = in_ref[at : at + tokens]
    for y in range(2):
        b = pl.ds((3 * y + 2) * HD, HD)
        for i in range(2):
            at = tokens + half + (2 * i + 1) * tokens

            def load(x):
                entry = lax.bitwise_xor(col, 2 * y + x)
                block = in_refs[0][at : at + tokens].astype(F32)
                for j in range(1, COLS):
                    block = jnp.where(entry == j, in_refs[j][at : at + tokens].astype(F32), block)
                return block

            out_refs[1 + i][:, b] = (load(0) + load(1)).astype(BF16)


def unpack(blocks, tokens, width):
    return pl.pallas_call(
        unpack_kernel,
        out_shape=[jax.ShapeDtypeStruct((tokens, width), BF16)] * 3,
        cost_estimate=SMALL,
        name="unpack_outputs",
    )(*blocks)


def hold_kernel(*refs):
    n = len(refs) // 2
    for in_ref, out_ref in zip(refs[:n], refs[n:]):
        out_ref[...] = in_ref[...]


def hold(blocks):
    return pl.pallas_call(
        hold_kernel,
        out_shape=[pltpu.VMEM(block.shape, block.dtype) for block in blocks],
        cost_estimate=SMALL,
        name="hold",
    )(*blocks)


def fence_kernel(in_ref, out_ref):
    del in_ref, out_ref


def fence(*earlier):
    mark = lax.optimization_barrier((jnp.zeros((8, 128), F32), earlier))[0]
    return pl.pallas_call(
        fence_kernel,
        in_specs=[pl.BlockSpec(memory_space=pl.ANY)],
        out_specs=pl.BlockSpec(memory_space=pl.ANY),
        out_shape=jax.ShapeDtypeStruct(mark.shape, mark.dtype),
        compiler_params=pltpu.CompilerParams(has_side_effects=True),
        cost_estimate=WINDOW,
        name="fence",
    )(mark)


def fence0(mark):
    return pl.pallas_call(
        fence_kernel,
        in_specs=[pl.BlockSpec(memory_space=pl.ANY)],
        out_specs=pl.BlockSpec(memory_space=pl.ANY),
        out_shape=jax.ShapeDtypeStruct((8, 128), F32),
        compiler_params=pltpu.CompilerParams(has_side_effects=True),
        cost_estimate=WINDOW,
        name="fence",
    )(mark)


def after(value, *earlier):
    return lax.optimization_barrier((value, earlier))[0]


def per_device_fast(queries, keys_tile, values_tile, out_weight, out_grad):
    tokens = queries.shape[0]
    half = tokens // 2
    own = PLANES * tokens
    width = out_weight.shape[0]
    row, col = lax.axis_index("row"), lax.axis_index("col")
    plane, core = row // CORES, row % CORES

    def head(block, g):
        return block[:, g * HD : (g + 1) * HD]

    def to_col(block, j):
        return lax.ppermute(block, "col", col_xor(j))

    def to_plane(block, s):
        return lax.ppermute(block, "row", row_shift(s))

    def swap(block):
        return lax.ppermute(block, "row", SWAP)

    grad_1 = to_plane(out_grad, 1)
    grad_3 = to_plane(out_grad, -1)
    weights = (out_weight, swap(out_weight))

    pieces = pack(*after((queries, keys_tile, values_tile), fence0(queries)))
    pieces = after(pieces, weights[1])
    moved = after([to_col(pieces[j], j) for j in (1, 2, 3)], fence(pieces))
    weights = hold(weights)
    over_col = jnp.stack([pieces[0], *after(moved, weights)])

    arrived = [pick(over_col, col ^ plane)]
    for s in ORDER[1:]:
        arrived.append(to_plane(pick(over_col, col ^ ((plane + s) % PLANES)), s))

    early = grad_pieces((out_grad, grad_1, grad_3), *weights)
    early = list(early)
    early[1:] = [to_col(block, j) for j, block in enumerate(after(early[1:], arrived[1]), 1)]

    own_part = after(arrived, early)
    other_part = [swap(block) for block in (*arrived[:3], own_part[3])]
    other_part = after(other_part, fence(own_part))

    grad_2 = to_plane(after(grad_1, arrived), 1)
    grads = [out_grad, grad_1, grad_3, grad_2]

    probs, attn, q, k, v = attention_forward(own_part, other_part, tokens)
    grad_2 = after(grad_2, attn)
    early = [sum(t.astype(F32) for t in after(early, attn)).astype(BF16)]

    def plane_heads(rows, every):
        by_col = [pick(every, col ^ d) for d in range(COLS)]
        columns = []
        for y in range(2):
            columns += [by_col[2 * y][:rows], by_col[2 * y + 1][:rows]]
            halves = [by_col[2 * y + x][rows:].reshape(-1, half, HD) for x in range(2)]
            columns.append(jnp.concatenate(halves, axis=1).reshape(rows, HD))
        return jnp.concatenate(columns, axis=1)

    attn_a, attn_b = attn[:own], attn[own:]
    sent = jnp.concatenate([attn_a[3 * tokens :], attn_b[3 * half :]])
    late = grad_pieces((grad_2,), *weights)
    got = after([to_col(sent, j) for j in (1, 2, 3)], late)
    heads_2 = plane_heads(tokens, jnp.stack([sent, *got]))
    term_2 = mixed_term(heads_2, *weights, BF16)
    mixed_2 = to_plane(term_2, 1)
    late = [late[0]] + [to_col(late[j], j) for j in (1, 2, 3)]
    sent = jnp.concatenate([attn_a[: 3 * tokens], attn_b[: 3 * half]])
    pair = jnp.stack([sent, to_col(sent, 1)])
    rest = [pair, to_col(pair, 2)]

    dq, dkv, dkv_other = attention_backward(q, k, v, probs, attn, early, late)
    rest, mixed_2 = after((rest, mixed_2), dq)

    dkv_other = jnp.stack([jnp.stack([swap(dkv_other[i, h]) for h in range(2)]) for i in range(2)])
    dkv = dkv + dkv_other.astype(F32)
    dkv = dkv.astype(BF16).reshape(4, PLANES, tokens, HD)
    dq_a = dq[:own].reshape(PLANES, tokens, HD)
    dq_b = dq[own:].reshape(PLANES, half, HD)
    home = [
        jnp.concatenate([dq_a[p], dq_b[p]] + [dkv[i, p] for i in range(4)])
        for p in (ORDER.index(s) for s in range(PLANES))
    ]

    away = [to_plane(home[s], -s) for s in range(1, PLANES)]

    heads_rest = plane_heads(3 * tokens, jnp.concatenate(rest))
    heads = [heads_rest[p * tokens : (p + 1) * tokens] for p in range(3)] + [heads_2]
    ours, theirs = [
        [lax.dynamic_slice_in_dim(h, g * width, width, 1) for h in heads] for g in (core, 1 - core)
    ]
    total = weight_grad_part(after(theirs, home), grads)

    head_0, head_1, head_3 = after(heads[:3], total)
    term_1 = mixed_term(head_1, *weights, BF16)
    term_3 = (mixed_2.astype(F32) + mixed_term(head_3, *weights, F32)).astype(BF16)
    total = swap(total)
    term_0 = mixed_term(after(head_0, term_1, term_3), *weights, F32, WINDOW)

    away, total = after((away, total), term_0)
    home = [home[0], *away]
    weight_grad = weight_grad_part(after(ours, home), grads, total)

    mixed_1 = to_plane(after(term_1, home), -1)
    mixed_3 = to_plane(after(term_3, home), 1)

    home = after(jnp.stack(home), weight_grad)
    back = [pick(home, (col - plane) % PLANES)] + [
        to_col(pick(home, ((col ^ j) - plane) % PLANES), j) for j in (1, 2, 3)
    ]
    query_g, key_g, value_g = unpack(back, tokens, queries.shape[1])
    mixed_1, mixed_3 = after((mixed_1, mixed_3), query_g)
    mixed = (term_0 + mixed_1.astype(F32) + mixed_3.astype(F32)).astype(BF16)
    return (mixed, query_g, key_g, value_g, weight_grad)


def solution(mesh):
    spec = P("row", "col")
    fast = mesh.shape["row"] == PLANES * CORES and mesh.shape["col"] == COLS

    def run(queries, keys_tile, values_tile, out_weight, out_grad):
        heads = queries.shape[1] // HD
        fits = fast and heads == 6 * COLS and queries.shape[0] % (32 * mesh.shape["row"]) == 0
        return jax.shard_map(
            per_device_fast if fits else per_device,
            mesh=mesh,
            in_specs=(spec,) * 5,
            out_specs=(spec,) * 5,
            check_vma=False,
        )(queries, keys_tile, values_tile, out_weight, out_grad)

    return run
```
